32 devices in a mesh: group: 2 (over y), ctx: 4 (over z), feat: 2 (over x), ex: 2 (over core).
Axes of the slice: x: 2, y: 2, z: 4, core: 2. Of those that a mesh axis runs over, the one named last changes fastest.
Arguments:
- hidden: bfloat16 [8, 512, 8192], P(('group', 'feat', 'ex'), 'ctx'), parts along dimension 0, may hold values from -6 to 6
- cotangent: bfloat16 [8, 512, 1024], P(('group', 'feat', 'ex'), 'ctx'), parts along dimension 0, may hold values from -6 to 6
- adapter_down_factor: bfloat16 [8192, 16], replicated, may hold values from -0.0625 to 0.0625
- projection: bfloat16 [16384, 8192], P('ctx', 'feat'), may hold values from -6 to 6
- lengths: int32 [8], P(('group', 'feat', 'ex')), parts along dimension 0, may hold values from 128 to 512, as said below
- slot_example_order: int32 [8], P('group'), parts along dimension 0, may hold values from 0 to 3, each once
Outputs:
- features: float32 [8, 8192], P(('group', 'ex'), 'feat'), parts along dimension 0
The draws below stay inside these ranges and needn't reach their ends.
There are 2 independent parts, one for each index of `group`. The reference program is written for one: setup_inputs(seed, part) draws one part's arguments, and reference() takes and returns one part's arrays. A program takes and returns all parts, laid end to end along the dimension named above; an argument that names none is the same for every part. Nothing has to cross between parts.
Inputs may be any that keep to these rules, and one draw needn't show every extreme that they name: `lengths`: some example has exactly 512 valid positions and some exactly one quarter of 512.
All inputs are finite; a program needn't handle non-finite values.
Results may differ from the reference program's by a relative error of at most 0.0042.
Values may be sent and summed in bfloat16 or wider, within the bound.
A program may use at most 64 MiB of HBM per device.

```python
import jax
import jax.numpy as jnp
from jax import lax

MODEL_DIM = 8192
KVW = 1024
ADAPTER_RANK = 16
FEATS = 8192
GRAD = 16384
LEN = 512
NEX = 4


def draw_lengths(key, part):
    first_key, second_key = jax.random.split(jax.random.fold_in(key, 11))
    base = jax.random.randint(first_key, (NEX,), LEN // 4, LEN + 1)
    chosen = jax.random.permutation(second_key, NEX)
    base = base.at[chosen[0]].set(LEN)
    base = base.at[chosen[1]].set(LEN // 4)
    return base.astype(jnp.int32)


def draw_projection(key, part):
    keys = jax.random.split(jax.random.fold_in(key, 23), 2)
    ramp = jnp.arange(FEATS, dtype=jnp.float32) / FEATS
    jitter = jax.random.uniform(keys[0], (FEATS,), jnp.float32)
    column_entry = 10.0 ** (0.5 * ramp + 0.5 * jitter)
    entries = jnp.clip(jax.random.normal(keys[1], (GRAD, FEATS), jnp.float32), -4.5, 4.5)
    values = entries * column_entry[None, :] / jnp.sqrt(jnp.float32(GRAD))
    return jnp.clip(values, -6.0, 6.0).astype(jnp.bfloat16)


def block_scale(own_key, shape, shards, least, high):
    gain = 1.0
    for dim, shards_of in shards:
        heights = jax.random.uniform(jax.random.fold_in(jax.random.fold_in(own_key, 6), dim), (shards_of,), jnp.float32, least / len(shards), high / len(shards))
        gain = gain * jnp.repeat(jnp.exp(heights), shape[dim] // shards_of).reshape((-1,) + (1,) * (len(shape) - 1 - dim))
    return gain


def normal_values(stream_key, dims, deviation, bound, pieces=(), held_as=jnp.bfloat16):
    array = jax.random.normal(stream_key, dims, jnp.float32) * deviation
    if len(pieces) > 0:
        array = block_scale(stream_key, dims, pieces, -0.22, 0.18) * array
    return jnp.clip(array, min=-bound, max=bound).astype(held_as)


def setup_inputs(seed: int = 0, part: int = 0) -> dict:
    arg_keys = jax.random.split(jax.random.key(seed), 7)
    part_splits = jax.random.split(jax.random.fold_in(arg_keys[6], part), 7)
    hidden = normal_values(part_splits[0], (NEX, LEN, MODEL_DIM), 1.0, 6.0, ((0, 4), (1, 4)))
    cotangent = normal_values(part_splits[1], (NEX, LEN, KVW), 1.0, 6.0, ((0, 4), (1, 4)))
    adapter_down_factor = normal_values(arg_keys[2], (MODEL_DIM, ADAPTER_RANK), MODEL_DIM ** -0.5, 0.0625)
    projection = draw_projection(jax.random.fold_in(arg_keys[6], 71), part)
    lengths = draw_lengths(jax.random.fold_in(jax.random.fold_in(arg_keys[6], part), 71), part)
    slot_example_order = jax.random.permutation(part_splits[5], NEX).astype(jnp.int32)
    return dict(hidden=hidden, cotangent=cotangent, adapter_down_factor=adapter_down_factor, projection=projection, lengths=lengths, slot_example_order=slot_example_order)


def reference(hidden, cotangent, adapter_down_factor, projection, lengths, slot_example_order):
    flattened_rows = hidden.reshape(NEX * LEN, MODEL_DIM)
    down_factor_rows = jnp.dot(flattened_rows, adapter_down_factor, preferred_element_type=jnp.float32).astype(jnp.bfloat16)
    down_factor_rows = down_factor_rows.reshape(NEX, LEN, ADAPTER_RANK)
    position = jnp.arange(LEN, dtype=jnp.int32)
    retain_mask = (position[None, :] < lengths[:, None]).astype(jnp.bfloat16)
    down_factor_rows = down_factor_rows * retain_mask[:, :, None]
    grad = jnp.einsum('ntr,ntj->nrj', down_factor_rows.astype(jnp.float32), cotangent.astype(jnp.float32))
    grad_rows = grad.reshape(NEX, GRAD).astype(jnp.bfloat16)
    projected = jnp.dot(grad_rows, projection, preferred_element_type=jnp.float32)
    scaled = projected / jnp.sqrt(lax.optimization_barrier(jnp.mean(projected * projected, axis=1, keepdims=True)) + 1e-06)
    example_ids = jnp.arange(NEX, dtype=jnp.int32)
    select = (slot_example_order[None, :] == example_ids[:, None]).astype(jnp.float32)
    return jnp.dot(select, scaled, precision=lax.Precision.HIGHEST, preferred_element_type=jnp.float32)
```

```python
import functools

import jax
import jax.numpy as jnp
from jax import lax
from jax.experimental import pallas as pl
from jax.experimental.pallas import tpu as pltpu
from jax.sharding import PartitionSpec as P

MESH = pl.DeviceIdType.MESH
F32 = jnp.float32
BF16 = jnp.bfloat16
FEATS = 8192
LANES = 128
HIDDEN_CHUNKS = 4


def loop(low, high, body):
    if high - low <= 4:
        for step in range(low, high):
            body(step)
    else:
        lax.fori_loop(low, high, lambda step, carry: (body(step), carry)[1], 0)


def kernel(
    sizes,
    lengths_ref, order_ref, hidden_ref, cotangent_ref, factor_ref, projection_ref,
    out_ref,
    hidden_v, cotangent_v, factor_v, projection_v,
    partial, partial_in, grads, grad_rows, rows_out, rows_in, final_out, final_in, squares_in,
    local_sem, projection_sem,
    grad_send, grad_recv, gather_send, gather_recv, rows_send, rows_recv,
    final_send, final_recv, squares_send, squares_recv,
):
    ctx_count, feat_count, ex_count = sizes
    ctx, feat, ex = lax.axis_index("ctx"), lax.axis_index("feat"), lax.axis_index("ex")
    slots = feat_count * ex_count
    slot = feat * ex_count + ex
    token_count, model_width = hidden_v.shape
    rank = factor_v.shape[0]
    own_rank = rank // ctx_count
    chunk_count, depth, chunk = projection_v.shape
    width = chunk_count * chunk
    value_width = cotangent_v.shape[1]
    padded = max(8, slots)
    own_ids = out_ref.shape[0]

    step = model_width // HIDDEN_CHUNKS
    factor_copy = pltpu.make_async_copy(factor_ref, factor_v, local_sem.at[0])
    factor_copy.start()
    hidden_copies = []
    for k in range(HIDDEN_CHUNKS):
        columns = pl.ds(k * step, step)
        hidden_copies.append(
            pltpu.make_async_copy(
                hidden_ref.at[0, :, columns], hidden_v.at[:, columns], local_sem.at[2 + k]
            )
        )
        hidden_copies[-1].start()
    cotangent_copy = pltpu.make_async_copy(cotangent_ref.at[0], cotangent_v, local_sem.at[1])
    cotangent_copy.start()
    projection_copies = []
    for k in range(chunk_count):
        columns = pl.ds(pl.multiple_of(ex * width + k * chunk, LANES), chunk)
        projection_copies.append(
            pltpu.make_async_copy(
                projection_ref.at[:, columns], projection_v.at[k], projection_sem.at[k]
            )
        )
        projection_copies[-1].start()

    barrier = pltpu.get_barrier_semaphore()
    members = ctx_count * slots
    me = ctx * slots + slot

    def greet(d):
        other = lax.rem(me + d, members)
        pl.semaphore_signal(
            barrier, inc=1, device_id_type=MESH,
            device_id={
                "ctx": other // slots,
                "feat": lax.rem(other // ex_count, feat_count),
                "ex": lax.rem(other, ex_count),
            },
        )

    loop(1, members, greet)

    pick_shape = (own_rank * padded, slots * own_rank)
    row, column = lax.broadcasted_iota(jnp.int32, pick_shape, 0), lax.broadcasted_iota(jnp.int32, pick_shape, 1)
    column_id = jnp.zeros(pick_shape, jnp.int32)
    for s in range(slots):
        column_id = jnp.where(column // own_rank == s, order_ref[s], column_id)
    pick = (row // padded == lax.rem(column, own_rank)) & (lax.rem(row, padded) == column_id)
    pick = pick.astype(F32).astype(BF16)

    factor_copy.wait()
    down = jnp.zeros((rank, token_count), F32)
    for k in range(HIDDEN_CHUNKS):
        hidden_copies[k].wait()
        columns = pl.ds(k * step, step)
        down += lax.dot_general(
            factor_v[:, columns], hidden_v[:, columns], (((1,), (1,)), ((), ())),
            preferred_element_type=F32,
        )
    position = ctx * token_count + lax.broadcasted_iota(jnp.int32, down.shape, 1)
    down = jnp.where(position < lengths_ref[0], down, 0.0).astype(BF16)
    cotangent_copy.wait()
    grad = jnp.dot(down, cotangent_v[...], preferred_element_type=F32)
    for k in range(ctx_count):
        partial[k] = grad[k * own_rank:(k + 1) * own_rank]

    pl.semaphore_wait(barrier, members - 1)

    def grad_copy(d):
        other = lax.rem(ctx + d, ctx_count)
        return pltpu.make_async_remote_copy(
            src_ref=partial.at[other], dst_ref=partial_in.at[ctx],
            send_sem=grad_send.at[d], recv_sem=grad_recv.at[ctx],
            device_id={"ctx": other}, device_id_type=MESH,
        )

    def grad_arrival(d):
        other = lax.rem(ctx + d, ctx_count)
        pltpu.make_async_remote_copy(
            src_ref=partial.at[other], dst_ref=partial_in.at[other],
            send_sem=grad_send.at[d], recv_sem=grad_recv.at[other],
            device_id={"ctx": other}, device_id_type=MESH,
        ).wait_recv()

    loop(1, ctx_count, lambda d: grad_copy(d).start())
    partial_in[ctx] = partial[ctx]
    loop(1, ctx_count, grad_arrival)
    total = partial_in[0]
    for k in range(1, ctx_count):
        total += partial_in[k]
    grads[slot] = total.astype(BF16).astype(F32)

    def gather_copy(d):
        other = lax.rem(slot + d, slots)
        return pltpu.make_async_remote_copy(
            src_ref=grads.at[slot], dst_ref=grads.at[slot],
            send_sem=gather_send.at[d], recv_sem=gather_recv.at[slot],
            device_id={"feat": other // ex_count, "ex": lax.rem(other, ex_count)},
            device_id_type=MESH,
        )

    def gather_arrival(d):
        other = lax.rem(slot + d, slots)
        pltpu.make_async_remote_copy(
            src_ref=grads.at[other], dst_ref=grads.at[other],
            send_sem=gather_send.at[d], recv_sem=gather_recv.at[other],
            device_id={"feat": other // ex_count, "ex": lax.rem(other, ex_count)},
            device_id_type=MESH,
        ).wait_recv()

    loop(1, slots, lambda d: gather_copy(d).start())
    loop(1, slots, gather_arrival)
    for s in range(slots):
        grad_rows[s * own_rank:(s + 1) * own_rank] = grads[s]
    picked = jnp.dot(pick, grad_rows[...].astype(BF16), preferred_element_type=F32)
    left = [picked[r * padded:(r + 1) * padded].astype(BF16) for r in range(own_rank)]

    for k in range(chunk_count):
        projection_copies[k].wait()
        product = jnp.zeros((padded, chunk), F32)
        for r in range(own_rank):
            product += jnp.dot(
                left[r], projection_v[k, r * value_width:(r + 1) * value_width, :],
                preferred_element_type=F32,
            )
        for i in range(slots):
            rows_out[i, :, k * chunk:(k + 1) * chunk] = product[i:i + 1]

    def rows_copy(d):
        other = lax.rem(ctx + d, ctx_count)
        return pltpu.make_async_remote_copy(
            src_ref=rows_out.at[other], dst_ref=rows_in.at[ctx],
            send_sem=rows_send.at[d], recv_sem=rows_recv.at[ctx],
            device_id={"ctx": other}, device_id_type=MESH,
        )

    def rows_arrival(d):
        other = lax.rem(ctx + d, ctx_count)
        pltpu.make_async_remote_copy(
            src_ref=rows_out.at[other], dst_ref=rows_in.at[other],
            send_sem=rows_send.at[d], recv_sem=rows_recv.at[other],
            device_id={"ctx": other}, device_id_type=MESH,
        ).wait_recv()

    loop(1, ctx_count, lambda d: rows_copy(d).start())
    rows_in[ctx] = rows_out[ctx]
    loop(1, ctx_count, rows_arrival)
    summed = rows_in[0]
    for k in range(1, ctx_count):
        summed += rows_in[k]
    square = jnp.sum(summed * summed, axis=1, keepdims=True)
    final_out[:, :width] = summed
    final_out[:, width:] = jnp.broadcast_to(square, (1, LANES))

    owner_ex = ctx // own_ids
    place = lax.rem(ctx, own_ids)
    tail = pl.ds(width, LANES)

    def final_copy(d):
        return pltpu.make_async_remote_copy(
            src_ref=final_out, dst_ref=final_in.at[place * ex_count + ex],
            send_sem=final_send.at[d], recv_sem=final_recv.at[place * ex_count + ex],
            device_id={"ctx": lax.rem(ctx + d, ctx_count), "ex": owner_ex},
            device_id_type=MESH,
        )

    def squares_copy(q):
        d, g = q // (feat_count - 1), lax.rem(q, feat_count - 1) + 1
        return pltpu.make_async_remote_copy(
            src_ref=final_out.at[:, tail],
            dst_ref=squares_in.at[feat, place * ex_count + ex],
            send_sem=squares_send.at[q], recv_sem=squares_recv.at[feat, place * ex_count + ex],
            device_id={
                "ctx": lax.rem(ctx + d, ctx_count),
                "feat": lax.rem(feat + g, feat_count),
                "ex": owner_ex,
            },
            device_id_type=MESH,
        )

    def final_arrival(q):
        pltpu.make_async_remote_copy(
            src_ref=final_out, dst_ref=final_in.at[q],
            send_sem=final_send.at[0], recv_sem=final_recv.at[q],
            device_id={"ctx": lax.rem(ctx + 1, ctx_count)}, device_id_type=MESH,
        ).wait_recv()

    def squares_arrival(q):
        g, source = q // (own_ids * ex_count) + 1, lax.rem(q, own_ids * ex_count)
        other = lax.rem(feat + g, feat_count)
        pltpu.make_async_remote_copy(
            src_ref=final_out.at[:, tail], dst_ref=squares_in.at[other, source],
            send_sem=squares_send.at[0], recv_sem=squares_recv.at[other, source],
            device_id={"feat": other}, device_id_type=MESH,
        ).wait_recv()

    square_sends = ctx_count * (feat_count - 1)
    owner = owner_ex == ex
    mine = place * ex_count + ex
    loop(0, square_sends, lambda q: squares_copy(q).start())
    loop(1, ctx_count, lambda d: final_copy(d).start())

    @pl.when(jnp.logical_not(owner))
    def _():
        final_copy(0).start()

    @pl.when(owner)
    def _():
        final_in[mine] = final_out[...]

    def arrive(q):
        @pl.when(jnp.logical_not(owner & (mine == q)))
        def _():
            final_arrival(q)

    loop(0, own_ids * ex_count, arrive)
    loop(0, (feat_count - 1) * own_ids * ex_count, squares_arrival)
    squares_in[feat] = final_in[:, :, width:]
    for i in range(own_ids):
        everything = squares_in[0, i * ex_count]
        for q in range(1, feat_count * ex_count):
            everything += squares_in[q // ex_count, i * ex_count + q % ex_count]
        norm = jnp.sqrt(everything[:, :1] / FEATS + 1e-06)
        for k in range(ex_count):
            out_ref[i:i + 1, k * width:(k + 1) * width] = final_in[i * ex_count + k, :, :width] / norm

    loop(1, ctx_count, lambda d: grad_copy(d).wait_send())
    loop(1, slots, lambda d: gather_copy(d).wait_send())
    loop(1, ctx_count, lambda d: rows_copy(d).wait_send())
    loop(1, ctx_count, lambda d: final_copy(d).wait_send())
    loop(0, square_sends, lambda q: squares_copy(q).wait_send())

    @pl.when(jnp.logical_not(owner))
    def _():
        final_copy(0).wait_send()


def per_device(sizes, hidden, cotangent, adapter_down_factor, projection, lengths, slot_example_order):
    ctx_count, feat_count, ex_count = sizes
    slots = feat_count * ex_count
    example_count, token_count, model_width = hidden.shape
    value_width = cotangent.shape[2]
    rank = adapter_down_factor.shape[1]
    depth, columns = projection.shape
    width = columns // ex_count
    chunk = min(512, width)
    own_ids = slots // ex_count
    own_rank = rank // ctx_count
    assert example_count == 1 and slots == ctx_count
    assert depth == own_rank * value_width
    dma = pltpu.SemaphoreType.DMA
    return pl.pallas_call(
        functools.partial(kernel, sizes),
        out_shape=jax.ShapeDtypeStruct((own_ids, columns), F32),
        in_specs=[pl.BlockSpec(memory_space=pltpu.SMEM)] * 2 + [pl.BlockSpec(memory_space=pl.ANY)] * 4,
        out_specs=pl.BlockSpec(memory_space=pltpu.VMEM),
        scratch_shapes=[
            pltpu.VMEM((token_count, model_width), BF16),
            pltpu.VMEM((token_count, value_width), BF16),
            pltpu.VMEM((rank, model_width), BF16),
            pltpu.VMEM((width // chunk, depth, chunk), BF16),
            pltpu.VMEM((ctx_count, own_rank, value_width), F32),
            pltpu.VMEM((ctx_count, own_rank, value_width), F32),
            pltpu.VMEM((slots, own_rank, value_width), F32),
            pltpu.VMEM((slots * own_rank, value_width), F32),
            pltpu.VMEM((slots, 1, width), F32),
            pltpu.VMEM((ctx_count, 1, width), F32),
            pltpu.VMEM((1, width + LANES), F32),
            pltpu.VMEM((own_ids * ex_count, 1, width + LANES), F32),
            pltpu.VMEM((feat_count, own_ids * ex_count, 1, LANES), F32),
            dma((2 + HIDDEN_CHUNKS,)),
            dma((width // chunk,)),
            dma((ctx_count,)),
            dma((ctx_count,)),
            dma((slots,)),
            dma((slots,)),
            dma((ctx_count,)),
            dma((ctx_count,)),
            dma((ctx_count,)),
            dma((own_ids * ex_count,)),
            dma((ctx_count * (feat_count - 1),)),
            dma((feat_count, own_ids * ex_count)),
        ],
        compiler_params=pltpu.CompilerParams(
            collective_id=0, has_side_effects=True, vmem_limit_bytes=48 * 1024 * 1024
        ),
    )(lengths, slot_example_order, hidden, cotangent, adapter_down_factor.T, projection)


def solution(mesh):
    in_specs = (
        P(("group", "feat", "ex"), "ctx", None),
        P(("group", "feat", "ex"), "ctx", None),
        P(),
        P("ctx", "feat"),
        P(("group", "feat", "ex")),
        P("group"),
    )
    out_specs = P(("group", "ex"), "feat")
    sizes = (mesh.shape["ctx"], mesh.shape["feat"], mesh.shape["ex"])
    return jax.shard_map(
        functools.partial(per_device, sizes),
        mesh=mesh, in_specs=in_specs, out_specs=out_specs, check_vma=False,
    )
```

```python
import functools

import jax
import jax.numpy as jnp
from jax import lax
from jax.experimental import pallas as pl
from jax.experimental.pallas import tpu as pltpu
from jax.sharding import PartitionSpec as P

MESH = pl.DeviceIdType.MESH
F32 = jnp.float32
BF16 = jnp.bfloat16
FEATS = 8192
LANES = 128
HIDDEN_CHUNKS = 4


def loop(low, high, body):
    if high - low <= 4:
        for step in range(low, high):
            body(step)
    else:
        lax.fori_loop(low, high, lambda step, carry: (body(step), carry)[1], 0)


def kernel(
    sizes,
    lengths_ref, order_ref, hidden_ref, cotangent_ref, factor_ref, projection_ref,
    out_ref,
    lengths_v, order_v, hidden_v, cotangent_v, factor_v, projection_v,
    partial, partial_in, grads, grad_rows, rows_out, rows_in, final_out, final_in, squares_in,
    local_sem, projection_sem,
    grad_send, grad_recv, gather_send, gather_recv, rows_send, rows_recv,
    final_send, final_recv, squares_send, squares_recv,
):
    ctx_count, feat_count, ex_count = sizes
    ctx, feat, ex = lax.axis_index("ctx"), lax.axis_index("feat"), lax.axis_index("ex")
    slots = feat_count * ex_count
    slot = feat * ex_count + ex
    token_count, model_width = hidden_v.shape
    rank = factor_v.shape[0]
    own_rank = rank // ctx_count
    chunk_count, depth, chunk = projection_v.shape
    width = chunk_count * chunk
    value_width = cotangent_v.shape[1]
    padded = max(8, slots)
    own_ids = out_ref.shape[0]
    halves, half_rows = rows_out.shape[:2]

    step = model_width // HIDDEN_CHUNKS
    factor_copy = pltpu.make_async_copy(factor_ref, factor_v, local_sem.at[0])
    factor_copy.start()
    hidden_copies = []
    for k in range(HIDDEN_CHUNKS):
        columns = pl.ds(k * step, step)
        hidden_copies.append(
            pltpu.make_async_copy(
                hidden_ref.at[0, :, columns], hidden_v.at[:, columns], local_sem.at[4 + k]
            )
        )
        hidden_copies[-1].start()
    order_copy = pltpu.make_async_copy(order_ref, order_v, local_sem.at[2])
    order_copy.start()
    lengths_copy = pltpu.make_async_copy(lengths_ref, lengths_v, local_sem.at[3])
    lengths_copy.start()
    cotangent_copy = pltpu.make_async_copy(cotangent_ref.at[0], cotangent_v, local_sem.at[1])
    cotangent_copy.start()
    projection_copies = []
    for k in range(chunk_count):
        columns = pl.ds(pl.multiple_of(ex * width + k * chunk, LANES), chunk)
        projection_copies.append(
            pltpu.make_async_copy(
                projection_ref.at[:, columns], projection_v.at[k], projection_sem.at[k]
            )
        )
        projection_copies[-1].start()

    def ctx_peer(d):
        return lax.rem(ctx + d, ctx_count)

    def slot_peer(d):
        other = lax.rem(slot + d, slots)
        return other, {"feat": other // ex_count, "ex": lax.rem(other, ex_count)}

    barrier = pltpu.get_barrier_semaphore()

    def greet_ctx(d):
        pl.semaphore_signal(
            barrier, inc=1, device_id_type=MESH, device_id={"ctx": ctx_peer(d)}
        )

    def greet_slot(d):
        pl.semaphore_signal(
            barrier, inc=1, device_id_type=MESH, device_id=slot_peer(d)[1]
        )

    loop(1, ctx_count, greet_ctx)
    loop(1, slots, greet_slot)

    order_copy.wait()
    pick_shape = (own_rank * padded, slots * own_rank)
    row = lax.broadcasted_iota(jnp.int32, pick_shape, 0)
    column = lax.broadcasted_iota(jnp.int32, pick_shape, 1)
    column_id = jnp.zeros(pick_shape, jnp.int32)
    for s in range(slots):
        column_id = jnp.where(column // own_rank == s, order_v[s], column_id)
    pick = (row // padded == lax.rem(column, own_rank)) & (lax.rem(row, padded) == column_id)
    pick = pick.astype(F32).astype(BF16)

    lengths_copy.wait()
    factor_copy.wait()
    down = jnp.zeros((rank, token_count), F32)
    for k in range(HIDDEN_CHUNKS):
        hidden_copies[k].wait()
        columns = pl.ds(k * step, step)
        down += lax.dot_general(
            factor_v[:, columns], hidden_v[:, columns], (((1,), (1,)), ((), ())),
            preferred_element_type=F32,
        )
    position = ctx * token_count + lax.broadcasted_iota(jnp.int32, down.shape, 1)
    down = jnp.where(position < lengths_v[0], down, 0.0).astype(BF16)
    cotangent_copy.wait()
    grad = jnp.dot(down, cotangent_v[...], preferred_element_type=F32)
    for k in range(ctx_count):
        partial[k] = grad[k * own_rank:(k + 1) * own_rank]

    pl.semaphore_wait(barrier, ctx_count - 1 + slots - 1)

    def grad_copy(d, landing=None):
        other = ctx_peer(d)
        source = ctx if landing is None else other
        return pltpu.make_async_remote_copy(
            src_ref=partial.at[other], dst_ref=partial_in.at[source],
            send_sem=grad_send.at[d], recv_sem=grad_recv.at[source],
            device_id={"ctx": other}, device_id_type=MESH,
        )

    loop(1, ctx_count, lambda d: grad_copy(d).start())
    partial_in[ctx] = partial[ctx]
    loop(1, ctx_count, lambda d: grad_copy(d, True).wait_recv())
    total = partial_in[0]
    for k in range(1, ctx_count):
        total += partial_in[k]
    grads[slot] = total.astype(BF16).astype(F32)

    def gather_copy(d, landing=None):
        other, device = slot_peer(d)
        source = slot if landing is None else other
        return pltpu.make_async_remote_copy(
            src_ref=grads.at[source], dst_ref=grads.at[source],
            send_sem=gather_send.at[d], recv_sem=gather_recv.at[source],
            device_id=device, device_id_type=MESH,
        )

    loop(1, slots, lambda d: gather_copy(d).start())
    loop(1, slots, lambda d: gather_copy(d, True).wait_recv())
    for s in range(slots):
        grad_rows[s * own_rank:(s + 1) * own_rank] = grads[s]
    picked = jnp.dot(pick, grad_rows[...].astype(BF16), preferred_element_type=F32)
    left = [picked[r * padded:(r + 1) * padded].astype(BF16) for r in range(own_rank)]

    def rows_copy(h, d, landing=None):
        other = ctx_peer(d)
        source = ctx if landing is None else other
        return pltpu.make_async_remote_copy(
            src_ref=rows_out.at[h], dst_ref=rows_in.at[source, h],
            send_sem=rows_send.at[h, d], recv_sem=rows_recv.at[h, source],
            device_id={"ctx": other}, device_id_type=MESH,
        )

    per_half = chunk_count // halves
    for h in range(halves):
        for j in range(per_half):
            k = h * per_half + j
            projection_copies[k].wait()
            product = jnp.zeros((padded, chunk), F32)
            for r in range(own_rank):
                product += jnp.dot(
                    left[r], projection_v[k, r * value_width:(r + 1) * value_width, :],
                    preferred_element_type=F32,
                )
            rows_out[h, j * slots:(j + 1) * slots] = product[:slots]
        loop(1, ctx_count, lambda d: rows_copy(h, d).start())
        rows_in[ctx, h] = rows_out[h]

    for h in range(halves):
        loop(1, ctx_count, lambda d: rows_copy(h, d, True).wait_recv())
        summed = rows_in[0, h]
        for k in range(1, ctx_count):
            summed += rows_in[k, h]
        square = jnp.broadcast_to(
            jnp.sum(summed * summed, axis=1, keepdims=True), (half_rows, LANES)
        )
        for j in range(per_half):
            k = h * per_half + j
            for x in range(ex_count):
                here = slice(j * slots + x * own_ids, j * slots + (x + 1) * own_ids)
                there = slice(k * own_ids, (k + 1) * own_ids)
                final_out[x, there, :chunk] = summed[here]
                final_out[x, there, chunk:] = square[here]

    tail = pl.ds(chunk, LANES)

    def final_copy(d, landing=None):
        other = lax.rem(ex + d, ex_count)
        source = ex if landing is None else other
        return pltpu.make_async_remote_copy(
            src_ref=final_out.at[other], dst_ref=final_in.at[source],
            send_sem=final_send.at[d], recv_sem=final_recv.at[source],
            device_id={"ex": other}, device_id_type=MESH,
        )

    def squares_copy(q, landing=None):
        g, x = q // ex_count + 1, lax.rem(ex + lax.rem(q, ex_count), ex_count)
        other = lax.rem(feat + g, feat_count)
        source = slot if landing is None else other * ex_count + x
        return pltpu.make_async_remote_copy(
            src_ref=final_out.at[x, :, tail], dst_ref=squares_in.at[source],
            send_sem=squares_send.at[q], recv_sem=squares_recv.at[source],
            device_id={"feat": other, "ex": x}, device_id_type=MESH,
        )

    square_sends = (feat_count - 1) * ex_count
    loop(0, square_sends, lambda q: squares_copy(q).start())
    loop(1, ex_count, lambda d: final_copy(d).start())
    final_in[ex] = final_out[ex]
    loop(1, ex_count, lambda d: final_copy(d, True).wait_recv())
    for x in range(ex_count):
        squares_in[feat * ex_count + x] = final_in[x, :, chunk:]
    loop(0, square_sends, lambda q: squares_copy(q, True).wait_recv())
    everything = squares_in[0]
    for s in range(1, slots):
        everything += squares_in[s]
    norm = everything[:own_ids, :1]
    for k in range(1, chunk_count):
        norm += everything[k * own_ids:(k + 1) * own_ids, :1]
    norm = jnp.sqrt(norm / FEATS + 1e-06)
    for x in range(ex_count):
        for k in range(chunk_count):
            place = x * width + k * chunk
            out_ref[:, place:place + chunk] = final_in[x, k * own_ids:(k + 1) * own_ids, :chunk] / norm

    loop(1, ctx_count, lambda d: grad_copy(d).wait_send())
    loop(1, slots, lambda d: gather_copy(d).wait_send())
    for h in range(halves):
        loop(1, ctx_count, lambda d: rows_copy(h, d).wait_send())
    loop(1, ex_count, lambda d: final_copy(d).wait_send())
    loop(0, square_sends, lambda q: squares_copy(q).wait_send())


def per_device(sizes, hidden, cotangent, adapter_down_factor, projection, lengths, slot_example_order):
    ctx_count, feat_count, ex_count = sizes
    slots = feat_count * ex_count
    example_count, token_count, model_width = hidden.shape
    value_width = cotangent.shape[2]
    rank = adapter_down_factor.shape[1]
    depth, columns = projection.shape
    width = columns // ex_count
    chunk = min(512, width)
    chunk_count = width // chunk
    halves = 2 if chunk_count % 2 == 0 else 1
    own_ids = slots // ex_count
    own_rank = rank // ctx_count
    assert example_count == 1 and depth == own_rank * value_width
    dma = pltpu.SemaphoreType.DMA
    return pl.pallas_call(
        functools.partial(kernel, sizes),
        out_shape=jax.ShapeDtypeStruct((own_ids, columns), F32),
        in_specs=[pl.BlockSpec(memory_space=pltpu.HBM)] * 6,
        out_specs=pl.BlockSpec(memory_space=pltpu.VMEM),
        scratch_shapes=[
            pltpu.SMEM(lengths.shape, jnp.int32),
            pltpu.SMEM(slot_example_order.shape, jnp.int32),
            pltpu.VMEM((token_count, model_width), BF16),
            pltpu.VMEM((token_count, value_width), BF16),
            pltpu.VMEM((rank, model_width), BF16),
            pltpu.VMEM((chunk_count, depth, chunk), BF16),
            pltpu.VMEM((ctx_count, own_rank, value_width), F32),
            pltpu.VMEM((ctx_count, own_rank, value_width), F32),
            pltpu.VMEM((slots, own_rank, value_width), F32),
            pltpu.VMEM((slots * own_rank, value_width), F32),
            pltpu.VMEM((halves, chunk_count * slots // halves, chunk), F32),
            pltpu.VMEM((ctx_count, halves, chunk_count * slots // halves, chunk), F32),
            pltpu.VMEM((ex_count, chunk_count * own_ids, chunk + LANES), F32),
            pltpu.VMEM((ex_count, chunk_count * own_ids, chunk + LANES), F32),
            pltpu.VMEM((slots, chunk_count * own_ids, LANES), F32),
            dma((4 + HIDDEN_CHUNKS,)),
            dma((chunk_count,)),
            dma((ctx_count,)),
            dma((ctx_count,)),
            dma((slots,)),
            dma((slots,)),
            dma((halves, ctx_count)),
            dma((halves, ctx_count)),
            dma((ex_count,)),
            dma((ex_count,)),
            dma(((feat_count - 1) * ex_count,)),
            dma((slots,)),
        ],
        compiler_params=pltpu.CompilerParams(
            collective_id=0, has_side_effects=True, vmem_limit_bytes=60 * 1024 * 1024
        ),
    )(lengths, slot_example_order, hidden, cotangent, adapter_down_factor.T, projection)


def solution(mesh):
    in_specs = (
        P(("group", "feat", "ex"), "ctx", None),
        P(("group", "feat", "ex"), "ctx", None),
        P(),
        P("ctx", "feat"),
        P(("group", "feat", "ex")),
        P("group"),
    )
    out_specs = P(("group", "ex"), "feat")
    sizes = (mesh.shape["ctx"], mesh.shape["feat"], mesh.shape["ex"])
    return jax.shard_map(
        functools.partial(per_device, sizes),
        mesh=mesh, in_specs=in_specs, out_specs=out_specs, check_vma=False,
    )
```

```python
import functools

import jax
import jax.numpy as jnp
from jax import lax
from jax.experimental import pallas as pl
from jax.experimental.pallas import tpu as pltpu
from jax.sharding import PartitionSpec as P

MESH = pl.DeviceIdType.MESH
F32 = jnp.float32
BF16 = jnp.bfloat16
LANES = 128
HIDDEN_CHUNKS = 4


def loop(low, high, body):
    if high - low <= 8:
        for step in range(low, high):
            body(step)
    else:
        lax.fori_loop(low, high, lambda step, carry: (body(step), carry)[1], 0)


def kernel(
    sizes,
    lengths_ref, order_ref, hidden_ref, cotangent_ref, factor_ref, projection_ref,
    out_ref,
    lengths_v, order_v, hidden_v, cotangent_v, factor_v, projection_v,
    ids, partial, partial_in, grads, rows_out, rows_in, final_out, final_in, squares_in,
    local_sem, projection_sem, ids_send, ids_recv,
    grad_send, grad_recv, gather_send, gather_recv, rows_send, rows_recv,
    final_send, final_recv, squares_send, squares_recv,
):
    group_count, ctx_count, feat_count, ex_count = sizes
    group, ctx, feat = lax.axis_index("group"), lax.axis_index("ctx"), lax.axis_index("feat")
    ex = lax.axis_index("ex")
    side_count = group_count * ex_count
    side = group * ex_count + ex
    slots = feat_count * side_count
    slot = feat * side_count + side
    group_slots = feat_count * ex_count
    token_count, model_width = hidden_v.shape
    rank = factor_v.shape[0]
    own_rank = rank // ctx_count
    chunk_count, depth, chunk = projection_v.shape
    width = chunk_count * chunk
    value_width = cotangent_v.shape[1]
    padded = max(8, slots)
    own_ids = out_ref.shape[0]
    halves, half_rows = rows_out.shape[:2]
    block, block_lanes = grads.shape[1:]
    pieces = value_width // block_lanes

    step = model_width // HIDDEN_CHUNKS
    factor_copy = pltpu.make_async_copy(factor_ref, factor_v, local_sem.at[0])
    factor_copy.start()
    hidden_copies = []
    for k in range(HIDDEN_CHUNKS):
        columns = pl.ds(k * step, step)
        hidden_copies.append(
            pltpu.make_async_copy(
                hidden_ref.at[0, :, columns], hidden_v.at[:, columns], local_sem.at[4 + k]
            )
        )
        hidden_copies[-1].start()
    order_copy = pltpu.make_async_copy(order_ref, order_v, local_sem.at[2])
    order_copy.start()
    lengths_copy = pltpu.make_async_copy(lengths_ref, lengths_v, local_sem.at[3])
    lengths_copy.start()
    cotangent_copy = pltpu.make_async_copy(cotangent_ref.at[0], cotangent_v, local_sem.at[1])
    cotangent_copy.start()
    projection_copies = []
    for k in range(chunk_count):
        columns = pl.ds(pl.multiple_of(side * width + k * chunk, LANES), chunk)
        projection_copies.append(
            pltpu.make_async_copy(
                projection_ref.at[:, columns], projection_v.at[k], projection_sem.at[k]
            )
        )

    def at_side(x):
        return {"group": x // ex_count, "ex": lax.rem(x, ex_count)}

    def ctx_peer(d):
        return lax.rem(ctx + d, ctx_count)

    def slot_peer(d):
        other = lax.rem(slot + d, slots)
        return other, {"feat": other // side_count, **at_side(lax.rem(other, side_count))}

    barrier = pltpu.get_barrier_semaphore()

    def greet_ctx(d):
        pl.semaphore_signal(
            barrier, inc=1, device_id_type=MESH, device_id={"ctx": ctx_peer(d)}
        )

    def greet_slot(d):
        pl.semaphore_signal(
            barrier, inc=1, device_id_type=MESH, device_id=slot_peer(d)[1]
        )

    loop(1, ctx_count, greet_ctx)
    loop(1, slots, greet_slot)

    order_copy.wait()
    lane = lax.broadcasted_iota(jnp.int32, ids.shape[1:], 1)
    own_order = jnp.zeros(ids.shape[1:], jnp.int32)
    for i in range(group_slots):
        own_order = jnp.where(lane == i, order_v[i], own_order)
    ids[group] = own_order

    lengths_copy.wait()
    factor_copy.wait()
    down = jnp.zeros((rank, token_count), F32)
    for k in range(HIDDEN_CHUNKS):
        hidden_copies[k].wait()
        if k == 1:
            for copy in projection_copies:
                copy.start()
        columns = pl.ds(k * step, step)
        down += lax.dot_general(
            factor_v[:, columns], hidden_v[:, columns], (((1,), (1,)), ((), ())),
            preferred_element_type=F32,
        )
    position = ctx * token_count + lax.broadcasted_iota(jnp.int32, down.shape, 1)
    down = jnp.where(position < lengths_v[0], down, 0.0).astype(BF16)
    cotangent_copy.wait()
    grad = jnp.dot(down, cotangent_v[...], preferred_element_type=F32)
    for k in range(ctx_count):
        partial[k] = grad[k * own_rank:(k + 1) * own_rank]

    pl.semaphore_wait(barrier, ctx_count - 1 + slots - 1)

    def grad_copy(d, landing=None):
        other = ctx_peer(d)
        source = ctx if landing is None else other
        return pltpu.make_async_remote_copy(
            src_ref=partial.at[other], dst_ref=partial_in.at[source],
            send_sem=grad_send.at[d], recv_sem=grad_recv.at[source],
            device_id={"ctx": other}, device_id_type=MESH,
        )

    def ids_copy(d, landing=None):
        other = lax.rem(group + d, group_count)
        source = group if landing is None else other
        return pltpu.make_async_remote_copy(
            src_ref=ids.at[source], dst_ref=ids.at[source],
            send_sem=ids_send.at[d], recv_sem=ids_recv.at[source],
            device_id={"group": other}, device_id_type=MESH,
        )

    loop(1, ctx_count, lambda d: grad_copy(d).start())
    loop(1, group_count, lambda d: ids_copy(d).start())
    partial_in[ctx] = partial[ctx]

    loop(1, group_count, lambda d: ids_copy(d, True).wait_recv())
    pick_shape = (own_rank * pieces * padded, slots * block)
    row = lax.broadcasted_iota(jnp.int32, pick_shape, 0)
    column = lax.broadcasted_iota(jnp.int32, pick_shape, 1)
    column_id = jnp.zeros(pick_shape, jnp.int32)
    for f in range(feat_count):
        for x in range(side_count):
            i = f * ex_count + x % ex_count
            value = ids[x // ex_count, :1, i:i + 1] + (x // ex_count) * group_slots
            column_id = jnp.where(column // block == f * side_count + x, value, column_id)
    wanted = lax.rem(row // padded, pieces) * own_rank + row // (padded * pieces)
    pick = (lax.rem(column, block) == wanted) & (lax.rem(row, padded) == column_id)
    pick = pick.astype(F32).astype(BF16)

    loop(1, ctx_count, lambda d: grad_copy(d, True).wait_recv())
    total = partial_in[0]
    for k in range(1, ctx_count):
        total += partial_in[k]
    rows = [total[:, q * block_lanes:(q + 1) * block_lanes] for q in range(pieces)]
    if pieces * own_rank < block:
        rows.append(jnp.zeros((block - pieces * own_rank, block_lanes), F32))
    grads[slot] = jnp.concatenate(rows, axis=0).astype(BF16)

    def gather_copy(d, landing=None):
        other, device = slot_peer(d)
        source = slot if landing is None else other
        return pltpu.make_async_remote_copy(
            src_ref=grads.at[source], dst_ref=grads.at[source],
            send_sem=gather_send.at[d], recv_sem=gather_recv.at[source],
            device_id=device, device_id_type=MESH,
        )

    loop(1, slots, lambda d: gather_copy(d).start())
    loop(1, slots, lambda d: gather_copy(d, True).wait_recv())
    gathered = grads[...].reshape(slots * block, block_lanes)
    picked = jnp.dot(pick, gathered, preferred_element_type=F32)
    left = [picked[i * padded:(i + 1) * padded].astype(BF16) for i in range(own_rank * pieces)]

    def rows_copy(h, d, landing=None):
        other = ctx_peer(d)
        source = ctx if landing is None else other
        return pltpu.make_async_remote_copy(
            src_ref=rows_out.at[h], dst_ref=rows_in.at[source, h],
            send_sem=rows_send.at[h, d], recv_sem=rows_recv.at[h, source],
            device_id={"ctx": other}, device_id_type=MESH,
        )

    per_half = chunk_count // halves
    for h in range(halves):
        for j in range(per_half):
            k = h * per_half + j
            projection_copies[k].wait()
            product = jnp.zeros((padded, chunk), F32)
            for i in range(own_rank * pieces):
                product += jnp.dot(
                    left[i], projection_v[k, i * block_lanes:(i + 1) * block_lanes, :],
                    preferred_element_type=F32,
                )
            rows_out[h, j * slots:(j + 1) * slots] = product[:slots]
        loop(1, ctx_count, lambda d: rows_copy(h, d).start())
        rows_in[ctx, h] = rows_out[h]

    for h in range(halves):
        loop(1, ctx_count, lambda d: rows_copy(h, d, True).wait_recv())
        summed = rows_in[0, h]
        for k in range(1, ctx_count):
            summed += rows_in[k, h]
        square = jnp.broadcast_to(
            jnp.sum(summed * summed, axis=1, keepdims=True), (half_rows, LANES)
        )
        for j in range(per_half):
            k = h * per_half + j
            for x in range(side_count):
                here = slice(j * slots + x * own_ids, j * slots + (x + 1) * own_ids)
                there = slice(k * own_ids, (k + 1) * own_ids)
                final_out[x, there, :chunk] = summed[here]
                final_out[x, there, chunk:] = square[here]

    tail = pl.ds(chunk, LANES)

    def final_copy(d, landing=None):
        other = lax.rem(side + d, side_count)
        source = side if landing is None else other
        return pltpu.make_async_remote_copy(
            src_ref=final_out.at[other], dst_ref=final_in.at[source],
            send_sem=final_send.at[d], recv_sem=final_recv.at[source],
            device_id=at_side(other), device_id_type=MESH,
        )

    def squares_copy(q, landing=None):
        g, x = q // side_count + 1, lax.rem(side + lax.rem(q, side_count), side_count)
        other = lax.rem(feat + g, feat_count)
        source = slot if landing is None else other * side_count + x
        return pltpu.make_async_remote_copy(
            src_ref=final_out.at[x, :, tail], dst_ref=squares_in.at[source],
            send_sem=squares_send.at[q], recv_sem=squares_recv.at[source],
            device_id={"feat": other, **at_side(x)}, device_id_type=MESH,
        )

    square_sends = (feat_count - 1) * side_count
    loop(0, square_sends, lambda q: squares_copy(q).start())
    loop(1, side_count, lambda d: final_copy(d).start())
    final_in[side] = final_out[side]
    loop(1, side_count, lambda d: final_copy(d, True).wait_recv())
    for x in range(side_count):
        squares_in[feat * side_count + x] = final_in[x, :, chunk:]
    loop(0, square_sends, lambda q: squares_copy(q, True).wait_recv())
    everything = squares_in[0]
    for s in range(1, slots):
        everything += squares_in[s]
    norm = everything[:own_ids, :1]
    for k in range(1, chunk_count):
        norm += everything[k * own_ids:(k + 1) * own_ids, :1]
    norm = jnp.sqrt(norm / (feat_count * side_count * width) + 1e-06)
    for x in range(side_count):
        for k in range(chunk_count):
            place = x * width + k * chunk
            out_ref[:, place:place + chunk] = final_in[x, k * own_ids:(k + 1) * own_ids, :chunk] / norm

    loop(1, ctx_count, lambda d: grad_copy(d).wait_send())
    loop(1, slots, lambda d: gather_copy(d).wait_send())
    for h in range(halves):
        loop(1, ctx_count, lambda d: rows_copy(h, d).wait_send())
    loop(1, group_count, lambda d: ids_copy(d).wait_send())
    loop(1, side_count, lambda d: final_copy(d).wait_send())
    loop(0, square_sends, lambda q: squares_copy(q).wait_send())


def per_device(sizes, hidden, cotangent, adapter_down_factor, projection, lengths, slot_example_order):
    group_count, ctx_count, feat_count, ex_count = sizes
    side_count = group_count * ex_count
    slots = feat_count * side_count
    example_count, token_count, model_width = hidden.shape
    value_width = cotangent.shape[2]
    rank = adapter_down_factor.shape[1]
    depth, columns = projection.shape
    width = columns // side_count
    chunk = min(512, width)
    chunk_count = width // chunk
    halves = 2 if chunk_count % 2 == 0 else 1
    own_ids = slots // side_count
    own_rank = rank // ctx_count
    block_lanes = max(LANES, own_rank * value_width // 16)
    block = -(-own_rank * value_width // block_lanes // 16) * 16
    assert example_count == 1 and depth == own_rank * value_width
    dma = pltpu.SemaphoreType.DMA
    return pl.pallas_call(
        functools.partial(kernel, sizes),
        out_shape=jax.ShapeDtypeStruct((own_ids, columns), F32),
        in_specs=[pl.BlockSpec(memory_space=pltpu.HBM)] * 6,
        out_specs=pl.BlockSpec(memory_space=pltpu.VMEM),
        scratch_shapes=[
            pltpu.SMEM(lengths.shape, jnp.int32),
            pltpu.SMEM(slot_example_order.shape, jnp.int32),
            pltpu.VMEM((token_count, model_width), BF16),
            pltpu.VMEM((token_count, value_width), BF16),
            pltpu.VMEM((rank, model_width), BF16),
            pltpu.VMEM((chunk_count, depth, chunk), BF16),
            pltpu.VMEM((group_count, 8, LANES), jnp.int32),
            pltpu.VMEM((ctx_count, own_rank, value_width), F32),
            pltpu.VMEM((ctx_count, own_rank, value_width), F32),
            pltpu.VMEM((slots, block, block_lanes), BF16),
            pltpu.VMEM((halves, chunk_count * slots // halves, chunk), F32),
            pltpu.VMEM((ctx_count, halves, chunk_count * slots // halves, chunk), F32),
            pltpu.VMEM((side_count, chunk_count * own_ids, chunk + LANES), F32),
            pltpu.VMEM((side_count, chunk_count * own_ids, chunk + LANES), F32),
            pltpu.VMEM((slots, chunk_count * own_ids, LANES), F32),
            dma((4 + HIDDEN_CHUNKS,)),
            dma((chunk_count,)),
            dma((group_count,)),
            dma((group_count,)),
            dma((ctx_count,)),
            dma((ctx_count,)),
            dma((slots,)),
            dma((slots,)),
            dma((halves, ctx_count)),
            dma((halves, ctx_count)),
            dma((side_count,)),
            dma((side_count,)),
            dma(((feat_count - 1) * side_count,)),
            dma((slots,)),
        ],
        compiler_params=pltpu.CompilerParams(
            collective_id=0, has_side_effects=True, vmem_limit_bytes=60 * 1024 * 1024
        ),
    )(lengths, slot_example_order, hidden, cotangent, adapter_down_factor.T, projection)


def solution(mesh):
    in_specs = (
        P(("group", "feat", "ex"), "ctx", None),
        P(("group", "feat", "ex"), "ctx", None),
        P(),
        P("ctx", "feat"),
        P(("group", "feat", "ex")),
        P("group"),
    )
    out_specs = P(("group", "ex"), "feat")
    sizes = (mesh.shape["group"], mesh.shape["ctx"], mesh.shape["feat"], mesh.shape["ex"])
    return jax.shard_map(
        functools.partial(per_device, sizes),
        mesh=mesh, in_specs=in_specs, out_specs=out_specs, check_vma=False,
    )
```

```python
import functools

import jax
import jax.numpy as jnp
from jax import lax
from jax.experimental import pallas as pl
from jax.experimental.pallas import tpu as pltpu
from jax.sharding import PartitionSpec as P

MESH = pl.DeviceIdType.MESH
F32 = jnp.float32
BF16 = jnp.bfloat16
LANES = 128
HIDDEN_CHUNKS = 4


def loop(low, high, body):
    if high - low <= 8:
        for step in range(low, high):
            body(step)
    else:
        lax.fori_loop(low, high, lambda step, carry: (body(step), carry)[1], 0)


def kernel(
    sizes,
    lengths_ref, order_ref, hidden_ref, cotangent_ref, factor_ref, projection_ref,
    out_ref,
    lengths_v, order_v, hidden_v, cotangent_v, factor_v, projection_v,
    ids, partial, partial_in, grads, rows_out, rows_in, final_out, final_in, squares_in,
    local_sem, projection_sem, ids_send, ids_recv,
    grad_send, grad_recv, gather_send, gather_recv, rows_send, rows_recv,
    final_send, final_recv, squares_send, squares_recv,
):
    group_count, ctx_count, feat_count, ex_count = sizes
    group, ctx, feat = lax.axis_index("group"), lax.axis_index("ctx"), lax.axis_index("feat")
    ex = lax.axis_index("ex")
    side_count = group_count * ex_count
    side = group * ex_count + ex
    slots = feat_count * side_count
    slot = feat * side_count + side
    group_slots = feat_count * ex_count
    token_count, model_width = hidden_v.shape
    rank = factor_v.shape[0]
    own_rank = rank // ctx_count
    chunk_count, depth, chunk = projection_v.shape
    width = chunk_count * chunk
    value_width = cotangent_v.shape[1]
    padded = max(8, slots)
    own_ids = out_ref.shape[0]
    block, block_lanes = grads.shape[1:]
    pieces = value_width // block_lanes

    step = model_width // HIDDEN_CHUNKS
    factor_copy = pltpu.make_async_copy(factor_ref, factor_v, local_sem.at[0])
    factor_copy.start()

    def hidden_copy(k):
        columns = pl.ds(pl.multiple_of(k * step, LANES), step)
        return pltpu.make_async_copy(
            hidden_ref.at[0, :, columns], hidden_v.at[:, columns], local_sem.at[4 + k]
        )

    for k in range(HIDDEN_CHUNKS):
        hidden_copy(k).start()
    order_copy = pltpu.make_async_copy(order_ref, order_v, local_sem.at[2])
    order_copy.start()
    lengths_copy = pltpu.make_async_copy(lengths_ref, lengths_v, local_sem.at[3])
    lengths_copy.start()
    cotangent_copy = pltpu.make_async_copy(cotangent_ref.at[0], cotangent_v, local_sem.at[1])
    cotangent_copy.start()

    def projection_copy(k):
        columns = pl.ds(pl.multiple_of(side * width + k * chunk, LANES), chunk)
        return pltpu.make_async_copy(
            projection_ref.at[:, columns], projection_v.at[k], projection_sem.at[k]
        )

    def at_side(x):
        return {"group": x // ex_count, "ex": lax.rem(x, ex_count)}

    def ctx_peer(d):
        return lax.rem(ctx + d, ctx_count)

    def slot_peer(d):
        other = lax.rem(slot + d, slots)
        return other, {"feat": other // side_count, **at_side(lax.rem(other, side_count))}

    barrier = pltpu.get_barrier_semaphore()

    def greet_ctx(d):
        pl.semaphore_signal(
            barrier, inc=1, device_id_type=MESH, device_id={"ctx": ctx_peer(d)}
        )

    def greet_slot(d):
        pl.semaphore_signal(
            barrier, inc=1, device_id_type=MESH, device_id=slot_peer(d)[1]
        )

    loop(1, ctx_count, greet_ctx)
    loop(1, slots, greet_slot)

    order_copy.wait()
    lane = lax.broadcasted_iota(jnp.int32, ids.shape[1:], 1)
    own_order = jnp.zeros(ids.shape[1:], jnp.int32)
    for i in range(group_slots):
        own_order = jnp.where(lane == i, order_v[i], own_order)
    ids[group] = own_order

    lengths_copy.wait()
    factor_copy.wait()
    hidden_copy(0).wait()
    for k in range(chunk_count):
        projection_copy(k).start()

    def add_down(k, down):
        @pl.when(k > 0)
        def _():
            hidden_copy(k).wait()

        columns = pl.ds(pl.multiple_of(k * step, LANES), step)
        return down + lax.dot_general(
            factor_v[:, columns], hidden_v[:, columns], (((1,), (1,)), ((), ())),
            preferred_element_type=F32,
        )

    down = lax.fori_loop(0, HIDDEN_CHUNKS, add_down, jnp.zeros((rank, token_count), F32))
    position = ctx * token_count + lax.broadcasted_iota(jnp.int32, down.shape, 1)
    down = jnp.where(position < lengths_v[0], down, 0.0).astype(BF16)
    cotangent_copy.wait()
    grad = jnp.dot(down, cotangent_v[...], preferred_element_type=F32)
    for k in range(ctx_count):
        partial[k] = grad[k * own_rank:(k + 1) * own_rank]

    pl.semaphore_wait(barrier, ctx_count - 1 + slots - 1)

    def grad_copy(d, landing=None):
        other = ctx_peer(d)
        source = ctx if landing is None else other
        return pltpu.make_async_remote_copy(
            src_ref=partial.at[other], dst_ref=partial_in.at[source],
            send_sem=grad_send.at[d], recv_sem=grad_recv.at[source],
            device_id={"ctx": other}, device_id_type=MESH,
        )

    def ids_copy(d, landing=None):
        other = lax.rem(group + d, group_count)
        source = group if landing is None else other
        return pltpu.make_async_remote_copy(
            src_ref=ids.at[source], dst_ref=ids.at[source],
            send_sem=ids_send.at[d], recv_sem=ids_recv.at[source],
            device_id={"group": other}, device_id_type=MESH,
        )

    loop(1, ctx_count, lambda d: grad_copy(d).start())
    loop(1, group_count, lambda d: ids_copy(d).start())
    partial_in[ctx] = partial[ctx]

    loop(1, group_count, lambda d: ids_copy(d, True).wait_recv())
    pick_shape = (own_rank * pieces * padded, slots * block)
    row = lax.broadcasted_iota(jnp.int32, pick_shape, 0)
    column = lax.broadcasted_iota(jnp.int32, pick_shape, 1)
    column_id = jnp.zeros(pick_shape, jnp.int32)
    for f in range(feat_count):
        for x in range(side_count):
            i = f * ex_count + x % ex_count
            value = ids[x // ex_count, :1, i:i + 1] + (x // ex_count) * group_slots
            column_id = jnp.where(column // block == f * side_count + x, value, column_id)
    wanted = lax.rem(row // padded, pieces) * own_rank + row // (padded * pieces)
    pick = (lax.rem(column, block) == wanted) & (lax.rem(row, padded) == column_id)
    pick = pick.astype(F32).astype(BF16)

    loop(1, ctx_count, lambda d: grad_copy(d, True).wait_recv())
    total = partial_in[0]
    for k in range(1, ctx_count):
        total += partial_in[k]
    rows = [total[:, q * block_lanes:(q + 1) * block_lanes] for q in range(pieces)]
    if pieces * own_rank < block:
        rows.append(jnp.zeros((block - pieces * own_rank, block_lanes), F32))
    grads[slot] = jnp.concatenate(rows, axis=0).astype(BF16)

    def gather_copy(d, landing=None):
        other, device = slot_peer(d)
        source = slot if landing is None else other
        return pltpu.make_async_remote_copy(
            src_ref=grads.at[source], dst_ref=grads.at[source],
            send_sem=gather_send.at[d], recv_sem=gather_recv.at[source],
            device_id=device, device_id_type=MESH,
        )

    loop(1, slots, lambda d: gather_copy(d).start())
    loop(1, slots, lambda d: gather_copy(d, True).wait_recv())
    gathered = grads[...].reshape(slots * block, block_lanes)
    picked = jnp.dot(pick, gathered, preferred_element_type=F32)
    left = [picked[i * padded:(i + 1) * padded].astype(BF16) for i in range(own_rank * pieces)]

    def rows_copy(h, d, landing=None):
        other = ctx_peer(d)
        source = ctx if landing is None else other
        return pltpu.make_async_remote_copy(
            src_ref=rows_out.at[h], dst_ref=rows_in.at[source, h],
            send_sem=rows_send.at[h, d], recv_sem=rows_recv.at[h, source],
            device_id={"ctx": other}, device_id_type=MESH,
        )

    def project(k, carry):
        projection_copy(k).wait()
        product = jnp.zeros((padded, chunk), F32)
        for i in range(own_rank * pieces):
            product += jnp.dot(
                left[i], projection_v[k, i * block_lanes:(i + 1) * block_lanes, :],
                preferred_element_type=F32,
            )
        rows_out[k] = product[:slots]
        for d in range(1, ctx_count):
            rows_copy(k, d).start()
        rows_in[ctx, k] = product[:slots]
        return carry

    lax.fori_loop(0, chunk_count, project, 0)

    for k in range(chunk_count):
        loop(1, ctx_count, lambda d: rows_copy(k, d, True).wait_recv())
        summed = rows_in[0, k]
        for c in range(1, ctx_count):
            summed += rows_in[c, k]
        square = jnp.broadcast_to(
            jnp.sum(summed * summed, axis=1, keepdims=True), (slots, LANES)
        )
        there = slice(k * own_ids, (k + 1) * own_ids)
        for x in range(side_count):
            here = slice(x * own_ids, (x + 1) * own_ids)
            final_out[x, there, :chunk] = summed[here]
            final_out[x, there, chunk:] = square[here]

    tail = pl.ds(chunk, LANES)

    def final_copy(d, landing=None):
        other = lax.rem(side + d, side_count)
        source = side if landing is None else other
        return pltpu.make_async_remote_copy(
            src_ref=final_out.at[other], dst_ref=final_in.at[source],
            send_sem=final_send.at[d], recv_sem=final_recv.at[source],
            device_id=at_side(other), device_id_type=MESH,
        )

    def squares_copy(q, landing=None):
        g, x = q // side_count + 1, lax.rem(side + lax.rem(q, side_count), side_count)
        other = lax.rem(feat + g, feat_count)
        source = slot if landing is None else other * side_count + x
        return pltpu.make_async_remote_copy(
            src_ref=final_out.at[x, :, tail], dst_ref=squares_in.at[source],
            send_sem=squares_send.at[q], recv_sem=squares_recv.at[source],
            device_id={"feat": other, **at_side(x)}, device_id_type=MESH,
        )

    square_sends = (feat_count - 1) * side_count
    loop(0, square_sends, lambda q: squares_copy(q).start())
    loop(1, side_count, lambda d: final_copy(d).start())
    final_in[side] = final_out[side]
    loop(1, side_count, lambda d: final_copy(d, True).wait_recv())
    for x in range(side_count):
        squares_in[feat * side_count + x] = final_in[x, :, chunk:]
    loop(0, square_sends, lambda q: squares_copy(q, True).wait_recv())
    everything = squares_in[0]
    for s in range(1, slots):
        everything += squares_in[s]
    norm = everything[:own_ids, :1]
    for k in range(1, chunk_count):
        norm += everything[k * own_ids:(k + 1) * own_ids, :1]
    norm = jnp.sqrt(norm / (feat_count * side_count * width) + 1e-06)
    for x in range(side_count):
        for k in range(chunk_count):
            place = x * width + k * chunk
            out_ref[:, place:place + chunk] = final_in[x, k * own_ids:(k + 1) * own_ids, :chunk] / norm

    loop(1, ctx_count, lambda d: grad_copy(d).wait_send())
    loop(1, slots, lambda d: gather_copy(d).wait_send())
    for k in range(chunk_count):
        loop(1, ctx_count, lambda d: rows_copy(k, d).wait_send())
    loop(1, group_count, lambda d: ids_copy(d).wait_send())
    loop(1, side_count, lambda d: final_copy(d).wait_send())
    loop(0, square_sends, lambda q: squares_copy(q).wait_send())


def per_device(sizes, hidden, cotangent, adapter_down_factor, projection, lengths, slot_example_order):
    group_count, ctx_count, feat_count, ex_count = sizes
    side_count = group_count * ex_count
    slots = feat_count * side_count
    example_count, token_count, model_width = hidden.shape
    value_width = cotangent.shape[2]
    rank = adapter_down_factor.shape[1]
    depth, columns = projection.shape
    width = columns // side_count
    chunk = min(256, width)
    chunk_count = width // chunk
    own_ids = slots // side_count
    own_rank = rank // ctx_count
    block_lanes = max(LANES, own_rank * value_width // 16)
    block = -(-own_rank * value_width // block_lanes // 16) * 16
    assert example_count == 1 and depth == own_rank * value_width
    dma = pltpu.SemaphoreType.DMA
    return pl.pallas_call(
        functools.partial(kernel, sizes),
        out_shape=jax.ShapeDtypeStruct((own_ids, columns), F32),
        in_specs=[pl.BlockSpec(memory_space=pltpu.HBM)] * 6,
        out_specs=pl.BlockSpec(memory_space=pltpu.VMEM),
        scratch_shapes=[
            pltpu.SMEM(lengths.shape, jnp.int32),
            pltpu.SMEM(slot_example_order.shape, jnp.int32),
            pltpu.VMEM((token_count, model_width), BF16),
            pltpu.VMEM((token_count, value_width), BF16),
            pltpu.VMEM((rank, model_width), BF16),
            pltpu.VMEM((chunk_count, depth, chunk), BF16),
            pltpu.VMEM((group_count, 8, LANES), jnp.int32),
            pltpu.VMEM((ctx_count, own_rank, value_width), F32),
            pltpu.VMEM((ctx_count, own_rank, value_width), F32),
            pltpu.VMEM((slots, block, block_lanes), BF16),
            pltpu.VMEM((chunk_count, slots, chunk), F32),
            pltpu.VMEM((ctx_count, chunk_count, slots, chunk), F32),
            pltpu.VMEM((side_count, chunk_count * own_ids, chunk + LANES), F32),
            pltpu.VMEM((side_count, chunk_count * own_ids, chunk + LANES), F32),
            pltpu.VMEM((slots, chunk_count * own_ids, LANES), F32),
            dma((4 + HIDDEN_CHUNKS,)),
            dma((chunk_count,)),
            dma((group_count,)),
            dma((group_count,)),
            dma((ctx_count,)),
            dma((ctx_count,)),
            dma((slots,)),
            dma((slots,)),
            dma((chunk_count, ctx_count)),
            dma((chunk_count, ctx_count)),
            dma((side_count,)),
            dma((side_count,)),
            dma(((feat_count - 1) * side_count,)),
            dma((slots,)),
        ],
        compiler_params=pltpu.CompilerParams(
            collective_id=0, has_side_effects=True, vmem_limit_bytes=60 * 1024 * 1024
        ),
    )(lengths, slot_example_order, hidden, cotangent, adapter_down_factor.T, projection)


def solution(mesh):
    in_specs = (
        P(("group", "feat", "ex"), "ctx", None),
        P(("group", "feat", "ex"), "ctx", None),
        P(),
        P("ctx", "feat"),
        P(("group", "feat", "ex")),
        P("group"),
    )
    out_specs = P(("group", "ex"), "feat")
    sizes = (mesh.shape["group"], mesh.shape["ctx"], mesh.shape["feat"], mesh.shape["ex"])
    return jax.shard_map(
        functools.partial(per_device, sizes),
        mesh=mesh, in_specs=in_specs, out_specs=out_specs, check_vma=False,
    )
```

```python
import functools

import jax
import jax.numpy as jnp
from jax import lax
from jax.experimental import pallas as pl
from jax.experimental.pallas import tpu as pltpu
from jax.sharding import PartitionSpec as P

MESH = pl.DeviceIdType.MESH
F32 = jnp.float32
BF16 = jnp.bfloat16
LANES = 128
HIDDEN_CHUNKS = 4


def loop(low, high, body):
    if high - low <= 8:
        for step in range(low, high):
            body(step)
    else:
        lax.fori_loop(low, high, lambda step, carry: (body(step), carry)[1], 0)


def kernel(
    sizes,
    lengths_ref, order_ref, hidden_ref, cotangent_ref, factor_ref, projection_ref,
    out_ref,
    lengths_v, order_v, hidden_v, cotangent_v, factor_v, projection_v,
    ids, partial, partial_in, grads, rows_out, rows_in, final_out, final_in, squares_in,
    local_sem, projection_sem, ids_send, ids_recv,
    grad_send, grad_recv, gather_send, gather_recv, rows_send, rows_recv,
    final_send, final_recv, squares_send, squares_recv,
):
    group_count, ctx_count, feat_count, ex_count = sizes
    group, ctx, feat = lax.axis_index("group"), lax.axis_index("ctx"), lax.axis_index("feat")
    ex = lax.axis_index("ex")
    side_count = group_count * ex_count
    side = group * ex_count + ex
    slots = feat_count * side_count
    slot = feat * side_count + side
    group_slots = feat_count * ex_count
    token_count, model_width = hidden_v.shape
    rank = factor_v.shape[0]
    own_rank = rank // ctx_count
    chunk_count, depth, chunk = projection_v.shape
    width = chunk_count * chunk
    value_width = cotangent_v.shape[1]
    padded = max(8, slots)
    own_ids = out_ref.shape[0]
    block, block_lanes = grads.shape[1:]
    pieces = value_width // block_lanes

    step = model_width // HIDDEN_CHUNKS
    factor_copy = pltpu.make_async_copy(factor_ref, factor_v, local_sem.at[0])
    factor_copy.start()

    def hidden_copy(k):
        columns = pl.ds(pl.multiple_of(k * step, LANES), step)
        return pltpu.make_async_copy(
            hidden_ref.at[0, :, columns], hidden_v.at[:, columns], local_sem.at[4 + k]
        )

    for k in range(HIDDEN_CHUNKS):
        hidden_copy(k).start()
    order_copy = pltpu.make_async_copy(order_ref, order_v, local_sem.at[2])
    order_copy.start()
    lengths_copy = pltpu.make_async_copy(lengths_ref, lengths_v, local_sem.at[3])
    lengths_copy.start()
    cotangent_copy = pltpu.make_async_copy(cotangent_ref.at[0], cotangent_v, local_sem.at[1])
    cotangent_copy.start()

    def projection_copy(k):
        columns = pl.ds(pl.multiple_of(side * width + k * chunk, LANES), chunk)
        return pltpu.make_async_copy(
            projection_ref.at[:, columns], projection_v.at[k], projection_sem.at[k]
        )

    def at_side(x):
        return {"group": x // ex_count, "ex": lax.rem(x, ex_count)}

    def ctx_peer(d):
        return lax.rem(ctx + d, ctx_count)

    def slot_peer(d):
        other = lax.rem(slot + d, slots)
        return other, {"feat": other // side_count, **at_side(lax.rem(other, side_count))}

    barrier = pltpu.get_barrier_semaphore()

    def greet_ctx(d):
        pl.semaphore_signal(
            barrier, inc=1, device_id_type=MESH, device_id={"ctx": ctx_peer(d)}
        )

    def greet_slot(d):
        pl.semaphore_signal(
            barrier, inc=1, device_id_type=MESH, device_id=slot_peer(d)[1]
        )

    loop(1, ctx_count, greet_ctx)
    loop(1, slots, greet_slot)

    order_copy.wait()
    lane = lax.broadcasted_iota(jnp.int32, ids.shape[1:], 1)
    own_order = jnp.zeros(ids.shape[1:], jnp.int32)
    for i in range(group_slots):
        own_order = jnp.where(lane == i, order_v[i], own_order)
    ids[group] = own_order

    lengths_copy.wait()
    factor_copy.wait()
    hidden_copy(0).wait()
    for k in range(chunk_count):
        projection_copy(k).start()

    def add_down(k, down):
        @pl.when(k > 0)
        def _():
            hidden_copy(k).wait()

        columns = pl.ds(pl.multiple_of(k * step, LANES), step)
        return down + lax.dot_general(
            factor_v[:, columns], hidden_v[:, columns], (((1,), (1,)), ((), ())),
            preferred_element_type=F32,
        )

    down = lax.fori_loop(0, HIDDEN_CHUNKS, add_down, jnp.zeros((rank, token_count), F32))
    position = ctx * token_count + lax.broadcasted_iota(jnp.int32, down.shape, 1)
    down = jnp.where(position < lengths_v[0], down, 0.0).astype(BF16)
    cotangent_copy.wait()
    grad = jnp.dot(down, cotangent_v[...], preferred_element_type=F32)
    for k in range(ctx_count):
        partial[k] = grad[k * own_rank:(k + 1) * own_rank]

    pl.semaphore_wait(barrier, ctx_count - 1 + slots - 1)

    def grad_copy(d, landing=None):
        other = ctx_peer(d)
        source = ctx if landing is None else other
        return pltpu.make_async_remote_copy(
            src_ref=partial.at[other], dst_ref=partial_in.at[source],
            send_sem=grad_send.at[d], recv_sem=grad_recv.at[source],
            device_id={"ctx": other}, device_id_type=MESH,
        )

    def ids_copy(d, landing=None):
        other = lax.rem(group + d, group_count)
        source = group if landing is None else other
        return pltpu.make_async_remote_copy(
            src_ref=ids.at[source], dst_ref=ids.at[source],
            send_sem=ids_send.at[d], recv_sem=ids_recv.at[source],
            device_id={"group": other}, device_id_type=MESH,
        )

    loop(1, ctx_count, lambda d: grad_copy(d).start())
    loop(1, group_count, lambda d: ids_copy(d).start())
    partial_in[ctx] = partial[ctx]

    loop(1, group_count, lambda d: ids_copy(d, True).wait_recv())
    pick_shape = (own_rank * pieces * padded, slots * block)
    row = lax.broadcasted_iota(jnp.int32, pick_shape, 0)
    column = lax.broadcasted_iota(jnp.int32, pick_shape, 1)
    column_id = jnp.zeros(pick_shape, jnp.int32)
    for f in range(feat_count):
        for x in range(side_count):
            i = f * ex_count + x % ex_count
            value = ids[x // ex_count, :1, i:i + 1] + (x // ex_count) * group_slots
            column_id = jnp.where(column // block == f * side_count + x, value, column_id)
    wanted = lax.rem(row // padded, pieces) * own_rank + row // (padded * pieces)
    pick = (lax.rem(column, block) == wanted) & (lax.rem(row, padded) == column_id)
    pick = pick.astype(F32).astype(BF16)

    loop(1, ctx_count, lambda d: grad_copy(d, True).wait_recv())
    total = partial_in[0]
    for k in range(1, ctx_count):
        total += partial_in[k]
    rows = [total[:, q * block_lanes:(q + 1) * block_lanes] for q in range(pieces)]
    if pieces * own_rank < block:
        rows.append(jnp.zeros((block - pieces * own_rank, block_lanes), F32))
    grads[slot] = jnp.concatenate(rows, axis=0).astype(BF16)

    def gather_copy(d, landing=None):
        other, device = slot_peer(d)
        source = slot if landing is None else other
        return pltpu.make_async_remote_copy(
            src_ref=grads.at[source], dst_ref=grads.at[source],
            send_sem=gather_send.at[d], recv_sem=gather_recv.at[source],
            device_id=device, device_id_type=MESH,
        )

    loop(1, slots, lambda d: gather_copy(d).start())
    loop(1, slots, lambda d: gather_copy(d, True).wait_recv())
    gathered = grads[...].reshape(slots * block, block_lanes)
    picked = jnp.dot(pick, gathered, preferred_element_type=F32)
    left = [picked[i * padded:(i + 1) * padded].astype(BF16) for i in range(own_rank * pieces)]

    def rows_copy(h, d, landing=None):
        other = ctx_peer(d)
        source = ctx if landing is None else other
        return pltpu.make_async_remote_copy(
            src_ref=rows_out.at[h], dst_ref=rows_in.at[source, h],
            send_sem=rows_send.at[h, d], recv_sem=rows_recv.at[h, source],
            device_id={"ctx": other}, device_id_type=MESH,
        )

    def project(k, carry):
        projection_copy(k).wait()
        product = jnp.zeros((padded, chunk), F32)
        for i in range(own_rank * pieces):
            product += jnp.dot(
                left[i], projection_v[k, i * block_lanes:(i + 1) * block_lanes, :],
                preferred_element_type=F32,
            )
        lanes = [product[:slots, p * LANES:(p + 1) * LANES] for p in range(chunk // LANES)]
        rows_out[k] = jnp.concatenate(lanes, axis=0).astype(BF16)
        for d in range(1, ctx_count):
            rows_copy(k, d).start()
        rows_in[ctx, k] = rows_out[k]
        return carry

    lax.fori_loop(0, chunk_count, project, 0)

    for k in range(chunk_count):
        loop(1, ctx_count, lambda d: rows_copy(k, d, True).wait_recv())
        summed = rows_in[0, k].astype(F32)
        for c in range(1, ctx_count):
            summed += rows_in[c, k].astype(F32)
        lanes = [summed[p * slots:(p + 1) * slots] for p in range(chunk // LANES)]
        square = lanes[0] * lanes[0]
        for part in lanes[1:]:
            square += part * part
        square = jnp.broadcast_to(jnp.sum(square, axis=1, keepdims=True), (slots, LANES))
        there = slice(k * own_ids, (k + 1) * own_ids)
        for x in range(side_count):
            here = slice(x * own_ids, (x + 1) * own_ids)
            for p, part in enumerate(lanes + [square]):
                final_out[x, there, p * LANES:(p + 1) * LANES] = part[here]

    tail = pl.ds(chunk, LANES)

    def final_copy(d, landing=None):
        other = lax.rem(side + d, side_count)
        source = side if landing is None else other
        return pltpu.make_async_remote_copy(
            src_ref=final_out.at[other], dst_ref=final_in.at[source],
            send_sem=final_send.at[d], recv_sem=final_recv.at[source],
            device_id=at_side(other), device_id_type=MESH,
        )

    def squares_copy(q, landing=None):
        g, x = q // side_count + 1, lax.rem(side + lax.rem(q, side_count), side_count)
        other = lax.rem(feat + g, feat_count)
        source = slot if landing is None else other * side_count + x
        return pltpu.make_async_remote_copy(
            src_ref=final_out.at[x, :, tail], dst_ref=squares_in.at[source],
            send_sem=squares_send.at[q], recv_sem=squares_recv.at[source],
            device_id={"feat": other, **at_side(x)}, device_id_type=MESH,
        )

    square_sends = (feat_count - 1) * side_count
    loop(0, square_sends, lambda q: squares_copy(q).start())
    loop(1, side_count, lambda d: final_copy(d).start())
    final_in[side] = final_out[side]
    loop(1, side_count, lambda d: final_copy(d, True).wait_recv())
    for x in range(side_count):
        squares_in[feat * side_count + x] = final_in[x, :, chunk:]
    loop(0, square_sends, lambda q: squares_copy(q, True).wait_recv())
    everything = squares_in[0]
    for s in range(1, slots):
        everything += squares_in[s]
    norm = everything[:own_ids, :1]
    for k in range(1, chunk_count):
        norm += everything[k * own_ids:(k + 1) * own_ids, :1]
    norm = jnp.sqrt(norm / (feat_count * side_count * width) + 1e-06)
    for x in range(side_count):
        for k in range(chunk_count):
            place = x * width + k * chunk
            out_ref[:, place:place + chunk] = final_in[x, k * own_ids:(k + 1) * own_ids, :chunk] / norm

    loop(1, ctx_count, lambda d: grad_copy(d).wait_send())
    loop(1, slots, lambda d: gather_copy(d).wait_send())
    for k in range(chunk_count):
        loop(1, ctx_count, lambda d: rows_copy(k, d).wait_send())
    loop(1, group_count, lambda d: ids_copy(d).wait_send())
    loop(1, side_count, lambda d: final_copy(d).wait_send())
    loop(0, square_sends, lambda q: squares_copy(q).wait_send())


def per_device(sizes, hidden, cotangent, adapter_down_factor, projection, lengths, slot_example_order):
    group_count, ctx_count, feat_count, ex_count = sizes
    side_count = group_count * ex_count
    slots = feat_count * side_count
    example_count, token_count, model_width = hidden.shape
    value_width = cotangent.shape[2]
    rank = adapter_down_factor.shape[1]
    depth, columns = projection.shape
    width = columns // side_count
    chunk = min(256, width)
    chunk_count = width // chunk
    own_ids = slots // side_count
    own_rank = rank // ctx_count
    block_lanes = max(LANES, own_rank * value_width // 16)
    block = -(-own_rank * value_width // block_lanes // 16) * 16
    assert example_count == 1 and depth == own_rank * value_width
    dma = pltpu.SemaphoreType.DMA
    return pl.pallas_call(
        functools.partial(kernel, sizes),
        out_shape=jax.ShapeDtypeStruct((own_ids, columns), F32),
        in_specs=[pl.BlockSpec(memory_space=pltpu.HBM)] * 6,
        out_specs=pl.BlockSpec(memory_space=pltpu.VMEM),
        scratch_shapes=[
            pltpu.SMEM(lengths.shape, jnp.int32),
            pltpu.SMEM(slot_example_order.shape, jnp.int32),
            pltpu.VMEM((token_count, model_width), BF16),
            pltpu.VMEM((token_count, value_width), BF16),
            pltpu.VMEM((rank, model_width), BF16),
            pltpu.VMEM((chunk_count, depth, chunk), BF16),
            pltpu.VMEM((group_count, 8, LANES), jnp.int32),
            pltpu.VMEM((ctx_count, own_rank, value_width), F32),
            pltpu.VMEM((ctx_count, own_rank, value_width), F32),
            pltpu.VMEM((slots, block, block_lanes), BF16),
            pltpu.VMEM((chunk_count, slots * chunk // LANES, LANES), BF16),
            pltpu.VMEM((ctx_count, chunk_count, slots * chunk // LANES, LANES), BF16),
            pltpu.VMEM((side_count, chunk_count * own_ids, chunk + LANES), F32),
            pltpu.VMEM((side_count, chunk_count * own_ids, chunk + LANES), F32),
            pltpu.VMEM((slots, chunk_count * own_ids, LANES), F32),
            dma((4 + HIDDEN_CHUNKS,)),
            dma((chunk_count,)),
            dma((group_count,)),
            dma((group_count,)),
            dma((ctx_count,)),
            dma((ctx_count,)),
            dma((slots,)),
            dma((slots,)),
            dma((chunk_count, ctx_count)),
            dma((chunk_count, ctx_count)),
            dma((side_count,)),
            dma((side_count,)),
            dma(((feat_count - 1) * side_count,)),
            dma((slots,)),
        ],
        compiler_params=pltpu.CompilerParams(
            collective_id=0, has_side_effects=True, vmem_limit_bytes=215 * 1024 * 256
        ),
    )(lengths, slot_example_order, hidden, cotangent, adapter_down_factor.T, projection)


def solution(mesh):
    in_specs = (
        P(("group", "feat", "ex"), "ctx", None),
        P(("group", "feat", "ex"), "ctx", None),
        P(),
        P("ctx", "feat"),
        P(("group", "feat", "ex")),
        P("group"),
    )
    out_specs = P(("group", "ex"), "feat")
    sizes = (mesh.shape["group"], mesh.shape["ctx"], mesh.shape["feat"], mesh.shape["ex"])
    return jax.shard_map(
        functools.partial(per_device, sizes),
        mesh=mesh, in_specs=in_specs, out_specs=out_specs, check_vma=False,
    )
```

```python
import functools

import jax
import jax.numpy as jnp
from jax import lax
from jax.experimental import pallas as pl
from jax.experimental.pallas import tpu as pltpu
from jax.sharding import PartitionSpec as P

MESH = pl.DeviceIdType.MESH
F32 = jnp.float32
BF16 = jnp.bfloat16
LANES = 128
HIDDEN_CHUNKS = 4


def loop(low, high, body):
    if high - low <= 16:
        for step in range(low, high):
            body(step)
    else:
        lax.fori_loop(low, high, lambda step, carry: (body(step), carry)[1], 0)


def kernel(
    sizes,
    lengths_ref, order_ref, hidden_ref, cotangent_ref, factor_ref, projection_ref,
    out_ref,
    lengths_v, order_v, hidden_v, cotangent_v, factor_v, projection_v,
    ids, partial, partial_in, grads, products, rows_out, rows_in, squares,
    local_sem, projection_sem, ids_send, ids_recv,
    grad_send, grad_recv, gather_send, gather_recv, rows_send, rows_recv,
    squares_send, squares_recv,
):
    group_count, ctx_count, feat_count, ex_count = sizes
    group, ctx, feat = lax.axis_index("group"), lax.axis_index("ctx"), lax.axis_index("feat")
    ex = lax.axis_index("ex")
    side_count = group_count * ex_count
    side = group * ex_count + ex
    slots = feat_count * side_count
    slot = feat * side_count + side
    group_slots = feat_count * ex_count
    token_count, model_width = hidden_v.shape
    rank = factor_v.shape[0]
    own_rank = rank // ctx_count
    chunk_count, depth, chunk = projection_v.shape
    width = chunk_count * chunk
    value_width = cotangent_v.shape[1]
    padded = max(8, slots)
    own_ids = out_ref.shape[0]
    block, block_lanes = grads.shape[1:]
    pieces = value_width // block_lanes

    step = model_width // HIDDEN_CHUNKS
    factor_copy = pltpu.make_async_copy(factor_ref, factor_v, local_sem.at[0])
    factor_copy.start()

    def hidden_copy(k):
        columns = pl.ds(pl.multiple_of(k * step, LANES), step)
        return pltpu.make_async_copy(
            hidden_ref.at[0, :, columns], hidden_v.at[:, columns], local_sem.at[4 + k]
        )

    for k in range(HIDDEN_CHUNKS):
        hidden_copy(k).start()
    order_copy = pltpu.make_async_copy(order_ref, order_v, local_sem.at[2])
    order_copy.start()
    lengths_copy = pltpu.make_async_copy(lengths_ref, lengths_v, local_sem.at[3])
    lengths_copy.start()
    cotangent_copy = pltpu.make_async_copy(cotangent_ref.at[0], cotangent_v, local_sem.at[1])
    cotangent_copy.start()

    def projection_copy(k):
        columns = pl.ds(pl.multiple_of(side * width + k * chunk, LANES), chunk)
        return pltpu.make_async_copy(
            projection_ref.at[:, columns], projection_v.at[k], projection_sem.at[k]
        )

    def at_side(x):
        return {"group": x // ex_count, "ex": lax.rem(x, ex_count)}

    def ctx_peer(d):
        return lax.rem(ctx + d, ctx_count)

    def slot_peer(d):
        other = lax.rem(slot + d, slots)
        return other, {"feat": other // side_count, **at_side(lax.rem(other, side_count))}

    def owner_peer(q):
        c = lax.rem(ctx + q // side_count, ctx_count)
        x = lax.rem(side + lax.rem(q, side_count), side_count)
        return c, x, {"ctx": c, **at_side(x)}

    barrier = pltpu.get_barrier_semaphore()

    def greet_owner(q):
        pl.semaphore_signal(
            barrier, inc=1, device_id_type=MESH, device_id=owner_peer(q)[2]
        )

    def greet_feat(q):
        other = lax.rem(feat + 1 + q // side_count, feat_count)
        pl.semaphore_signal(
            barrier, inc=1, device_id_type=MESH,
            device_id={"feat": other, **at_side(lax.rem(q, side_count))},
        )

    owners = ctx_count * side_count
    others = (feat_count - 1) * side_count
    loop(1, owners, greet_owner)
    loop(0, others, greet_feat)

    order_copy.wait()
    lane = lax.broadcasted_iota(jnp.int32, ids.shape[1:], 1)
    own_order = jnp.zeros(ids.shape[1:], jnp.int32)
    for i in range(group_slots):
        own_order = jnp.where(lane == i, order_v[i], own_order)
    ids[group] = own_order

    lengths_copy.wait()
    factor_copy.wait()
    hidden_copy(0).wait()
    for k in range(chunk_count):
        projection_copy(k).start()

    def add_down(k, down):
        @pl.when(k > 0)
        def _():
            hidden_copy(k).wait()

        columns = pl.ds(pl.multiple_of(k * step, LANES), step)
        return down + lax.dot_general(
            factor_v[:, columns], hidden_v[:, columns], (((1,), (1,)), ((), ())),
            preferred_element_type=F32,
        )

    down = lax.fori_loop(0, HIDDEN_CHUNKS, add_down, jnp.zeros((rank, token_count), F32))
    position = ctx * token_count + lax.broadcasted_iota(jnp.int32, down.shape, 1)
    down = jnp.where(position < lengths_v[0], down, 0.0).astype(BF16)
    cotangent_copy.wait()
    grad = jnp.dot(down, cotangent_v[...], preferred_element_type=F32)
    for k in range(ctx_count):
        partial[k] = grad[k * own_rank:(k + 1) * own_rank]

    pl.semaphore_wait(barrier, owners - 1 + others)

    def grad_copy(d, landing=None):
        other = ctx_peer(d)
        source = ctx if landing is None else other
        return pltpu.make_async_remote_copy(
            src_ref=partial.at[other], dst_ref=partial_in.at[source],
            send_sem=grad_send.at[d], recv_sem=grad_recv.at[source],
            device_id={"ctx": other}, device_id_type=MESH,
        )

    def ids_copy(d, landing=None):
        other = lax.rem(group + d, group_count)
        source = group if landing is None else other
        return pltpu.make_async_remote_copy(
            src_ref=ids.at[source], dst_ref=ids.at[source],
            send_sem=ids_send.at[d], recv_sem=ids_recv.at[source],
            device_id={"group": other}, device_id_type=MESH,
        )

    loop(1, ctx_count, lambda d: grad_copy(d).start())
    loop(1, group_count, lambda d: ids_copy(d).start())
    partial_in[ctx] = partial[ctx]

    loop(1, group_count, lambda d: ids_copy(d, True).wait_recv())
    pick_shape = (own_rank * pieces * padded, slots * block)
    row = lax.broadcasted_iota(jnp.int32, pick_shape, 0)
    column = lax.broadcasted_iota(jnp.int32, pick_shape, 1)
    column_id = jnp.zeros(pick_shape, jnp.int32)
    for f in range(feat_count):
        for x in range(side_count):
            i = f * ex_count + x % ex_count
            value = ids[x // ex_count, :1, i:i + 1] + (x // ex_count) * group_slots
            column_id = jnp.where(column // block == f * side_count + x, value, column_id)
    wanted = lax.rem(row // padded, pieces) * own_rank + row // (padded * pieces)
    pick = (lax.rem(column, block) == wanted) & (lax.rem(row, padded) == column_id)
    pick = pick.astype(F32).astype(BF16)

    loop(1, ctx_count, lambda d: grad_copy(d, True).wait_recv())
    total = partial_in[0]
    for k in range(1, ctx_count):
        total += partial_in[k]
    rows = [total[:, q * block_lanes:(q + 1) * block_lanes] for q in range(pieces)]
    if pieces * own_rank < block:
        rows.append(jnp.zeros((block - pieces * own_rank, block_lanes), F32))
    grads[slot] = jnp.concatenate(rows, axis=0).astype(BF16)

    def gather_copy(d, landing=None):
        other, device = slot_peer(d)
        source = slot if landing is None else other
        return pltpu.make_async_remote_copy(
            src_ref=grads.at[source], dst_ref=grads.at[source],
            send_sem=gather_send.at[d], recv_sem=gather_recv.at[source],
            device_id=device, device_id_type=MESH,
        )

    loop(1, slots, lambda d: gather_copy(d).start())
    loop(1, slots, lambda d: gather_copy(d, True).wait_recv())
    gathered = grads[...].reshape(slots * block, block_lanes)
    picked = jnp.dot(pick, gathered, preferred_element_type=F32)
    left = [picked[i * padded:(i + 1) * padded].astype(BF16) for i in range(own_rank * pieces)]

    def project(k, carry):
        projection_copy(k).wait()
        product = jnp.zeros((padded, chunk), F32)
        for i in range(own_rank * pieces):
            product += jnp.dot(
                left[i], projection_v[k, i * block_lanes:(i + 1) * block_lanes, :],
                preferred_element_type=F32,
            )
        products[k] = product[:slots]
        return carry

    lax.fori_loop(0, chunk_count, project, 0)

    def rows_copy(q, landing=None):
        c, x, device = owner_peer(q)
        source = (ctx, side) if landing is None else (c, x)
        return pltpu.make_async_remote_copy(
            src_ref=rows_out.at[x], dst_ref=rows_in.at[source[0], source[1]],
            send_sem=rows_send.at[q], recv_sem=rows_recv.at[source[0], source[1]],
            device_id=device, device_id_type=MESH,
        )

    tiles = chunk // LANES
    for x in range(side_count):
        rows_out[x] = jnp.concatenate(
            [
                products[k, x * own_ids:(x + 1) * own_ids, p * LANES:(p + 1) * LANES]
                for k in range(chunk_count) for p in range(tiles)
            ],
            axis=0,
        ).astype(BF16)
    loop(1, owners, lambda q: rows_copy(q).start())
    rows_in[ctx, side] = rows_out[side]
    loop(1, owners, lambda q: rows_copy(q, True).wait_recv())
    summed = []
    for x in range(side_count):
        summed.append(rows_in[0, x].astype(F32))
        for c in range(1, ctx_count):
            summed[x] += rows_in[c, x].astype(F32)

    square = summed[0] * summed[0]
    for part in summed[1:]:
        square += part * part
    square = jnp.sum(square, axis=1, keepdims=True)
    own_square = square[:own_ids]
    for t in range(1, chunk_count * tiles):
        own_square += square[t * own_ids:(t + 1) * own_ids]
    squares[feat] = jnp.broadcast_to(own_square, (own_ids, LANES))

    def squares_copy(d, landing=None):
        other = lax.rem(feat + d, feat_count)
        source = feat if landing is None else other
        return pltpu.make_async_remote_copy(
            src_ref=squares.at[source], dst_ref=squares.at[source],
            send_sem=squares_send.at[d], recv_sem=squares_recv.at[source],
            device_id={"feat": other}, device_id_type=MESH,
        )

    loop(1, feat_count, lambda d: squares_copy(d).start())
    loop(1, feat_count, lambda d: squares_copy(d, True).wait_recv())
    everything = squares[0]
    for f in range(1, feat_count):
        everything += squares[f]
    norm = jnp.sqrt(everything / (feat_count * side_count * width) + 1e-06)
    for x in range(side_count):
        for t in range(chunk_count * tiles):
            place = x * width + t * LANES
            out_ref[:, place:place + LANES] = summed[x][t * own_ids:(t + 1) * own_ids] / norm

    loop(1, ctx_count, lambda d: grad_copy(d).wait_send())
    loop(1, slots, lambda d: gather_copy(d).wait_send())
    loop(1, owners, lambda q: rows_copy(q).wait_send())
    loop(1, group_count, lambda d: ids_copy(d).wait_send())
    loop(1, feat_count, lambda d: squares_copy(d).wait_send())


def per_device(sizes, hidden, cotangent, adapter_down_factor, projection, lengths, slot_example_order):
    group_count, ctx_count, feat_count, ex_count = sizes
    side_count = group_count * ex_count
    slots = feat_count * side_count
    example_count, token_count, model_width = hidden.shape
    value_width = cotangent.shape[2]
    rank = adapter_down_factor.shape[1]
    depth, columns = projection.shape
    width = columns // side_count
    chunk = min(256, width)
    chunk_count = width // chunk
    own_ids = slots // side_count
    own_rank = rank // ctx_count
    block_lanes = max(LANES, own_rank * value_width // 16)
    block = -(-own_rank * value_width // block_lanes // 16) * 16
    assert example_count == 1 and depth == own_rank * value_width
    dma = pltpu.SemaphoreType.DMA
    return pl.pallas_call(
        functools.partial(kernel, sizes),
        out_shape=jax.ShapeDtypeStruct((own_ids, columns), F32),
        in_specs=[pl.BlockSpec(memory_space=pltpu.HBM)] * 6,
        out_specs=pl.BlockSpec(memory_space=pltpu.VMEM),
        scratch_shapes=[
            pltpu.SMEM(lengths.shape, jnp.int32),
            pltpu.SMEM(slot_example_order.shape, jnp.int32),
            pltpu.VMEM((token_count, model_width), BF16),
            pltpu.VMEM((token_count, value_width), BF16),
            pltpu.VMEM((rank, model_width), BF16),
            pltpu.VMEM((chunk_count, depth, chunk), BF16),
            pltpu.VMEM((group_count, 8, LANES), jnp.int32),
            pltpu.VMEM((ctx_count, own_rank, value_width), F32),
            pltpu.VMEM((ctx_count, own_rank, value_width), F32),
            pltpu.VMEM((slots, block, block_lanes), BF16),
            pltpu.VMEM((chunk_count, slots, chunk), F32),
            pltpu.VMEM((side_count, width // LANES * own_ids, LANES), BF16),
            pltpu.VMEM((ctx_count, side_count, width // LANES * own_ids, LANES), BF16),
            pltpu.VMEM((feat_count, own_ids, LANES), F32),
            dma((4 + HIDDEN_CHUNKS,)),
            dma((chunk_count,)),
            dma((group_count,)),
            dma((group_count,)),
            dma((ctx_count,)),
            dma((ctx_count,)),
            dma((slots,)),
            dma((slots,)),
            dma((ctx_count * side_count,)),
            dma((ctx_count, side_count)),
            dma((feat_count,)),
            dma((feat_count,)),
        ],
        compiler_params=pltpu.CompilerParams(
            collective_id=0, has_side_effects=True, vmem_limit_bytes=215 * 1024 * 256
        ),
    )(lengths, slot_example_order, hidden, cotangent, adapter_down_factor.T, projection)


def solution(mesh):
    in_specs = (
        P(("group", "feat", "ex"), "ctx", None),
        P(("group", "feat", "ex"), "ctx", None),
        P(),
        P("ctx", "feat"),
        P(("group", "feat", "ex")),
        P("group"),
    )
    out_specs = P(("group", "ex"), "feat")
    sizes = (mesh.shape["group"], mesh.shape["ctx"], mesh.shape["feat"], mesh.shape["ex"])
    return jax.shard_map(
        functools.partial(per_device, sizes),
        mesh=mesh, in_specs=in_specs, out_specs=out_specs, check_vma=False,
    )
```

```python
import functools

import jax
import jax.numpy as jnp
from jax import lax
from jax.experimental import pallas as pl
from jax.experimental.pallas import tpu as pltpu
from jax.sharding import PartitionSpec as P

MESH = pl.DeviceIdType.MESH
F32 = jnp.float32
BF16 = jnp.bfloat16
LANES = 128
HIDDEN_CHUNKS = 4


def loop(low, high, body):
    if high - low <= 8:
        for step in range(low, high):
            body(step)
    else:
        lax.fori_loop(low, high, lambda step, carry: (body(step), carry)[1], 0)


def kernel(
    sizes,
    lengths_ref, order_ref, hidden_ref, cotangent_ref, factor_ref, projection_ref,
    out_ref,
    lengths_v, order_v, hidden_v, cotangent_v, factor_v, projection_v,
    ids, partial, partial_in, grads, rows_out, rows_in, final_out, final_in, squares_in,
    local_sem, projection_sem, ids_send, ids_recv,
    grad_send, grad_recv, gather_send, gather_recv, rows_send, rows_recv,
    final_send, final_recv, squares_send, squares_recv,
):
    group_count, ctx_count, feat_count, ex_count = sizes
    group, ctx, feat = lax.axis_index("group"), lax.axis_index("ctx"), lax.axis_index("feat")
    ex = lax.axis_index("ex")
    side_count = group_count * ex_count
    side = group * ex_count + ex
    slots = feat_count * side_count
    slot = feat * side_count + side
    group_slots = feat_count * ex_count
    token_count, model_width = hidden_v.shape
    rank = factor_v.shape[0]
    own_rank = rank // ctx_count
    chunk_count, depth, chunk = projection_v.shape
    width = chunk_count * chunk
    value_width = cotangent_v.shape[1]
    padded = max(8, slots)
    own_ids = out_ref.shape[0]
    block, block_lanes = grads.shape[1:]
    pieces = value_width // block_lanes

    step = model_width // HIDDEN_CHUNKS
    factor_copy = pltpu.make_async_copy(factor_ref, factor_v, local_sem.at[0])
    factor_copy.start()

    def hidden_copy(k):
        columns = pl.ds(pl.multiple_of(k * step, LANES), step)
        return pltpu.make_async_copy(
            hidden_ref.at[0, :, columns], hidden_v.at[:, columns], local_sem.at[4 + k]
        )

    for k in range(HIDDEN_CHUNKS):
        hidden_copy(k).start()
    order_copy = pltpu.make_async_copy(order_ref, order_v, local_sem.at[2])
    order_copy.start()
    lengths_copy = pltpu.make_async_copy(lengths_ref, lengths_v, local_sem.at[3])
    lengths_copy.start()
    cotangent_copy = pltpu.make_async_copy(cotangent_ref.at[0], cotangent_v, local_sem.at[1])
    cotangent_copy.start()

    def projection_copy(k):
        columns = pl.ds(pl.multiple_of(side * width + k * chunk, LANES), chunk)
        return pltpu.make_async_copy(
            projection_ref.at[:, columns], projection_v.at[k], projection_sem.at[k]
        )

    def at_side(x):
        return {"group": x // ex_count, "ex": lax.rem(x, ex_count)}

    def ctx_peer(d):
        return lax.rem(ctx + d, ctx_count)

    def slot_peer(d):
        other = lax.rem(slot + d, slots)
        return other, {"feat": other // side_count, **at_side(lax.rem(other, side_count))}

    barrier = pltpu.get_barrier_semaphore()

    def greet_ctx(d):
        pl.semaphore_signal(
            barrier, inc=1, device_id_type=MESH, device_id={"ctx": ctx_peer(d)}
        )

    def greet_slot(d):
        pl.semaphore_signal(
            barrier, inc=1, device_id_type=MESH, device_id=slot_peer(d)[1]
        )

    loop(1, ctx_count, greet_ctx)
    loop(1, slots, greet_slot)

    order_copy.wait()
    lane = lax.broadcasted_iota(jnp.int32, ids.shape[1:], 1)
    own_order = jnp.zeros(ids.shape[1:], jnp.int32)
    for i in range(group_slots):
        own_order = jnp.where(lane == i, order_v[i], own_order)
    ids[group] = own_order

    lengths_copy.wait()
    factor_copy.wait()
    hidden_copy(0).wait()
    for k in range(chunk_count):
        projection_copy(k).start()

    def add_down(k, down):
        @pl.when(k > 0)
        def _():
            hidden_copy(k).wait()

        columns = pl.ds(pl.multiple_of(k * step, LANES), step)
        return down + lax.dot_general(
            hidden_v[:, columns], factor_v[:, columns], (((1,), (1,)), ((), ())),
            preferred_element_type=F32,
        )

    down = lax.fori_loop(0, HIDDEN_CHUNKS, add_down, jnp.zeros((token_count, rank), F32))
    position = ctx * token_count + lax.broadcasted_iota(jnp.int32, down.shape, 0)
    down = jnp.where(position < lengths_v[0], down, 0.0).astype(BF16)
    cotangent_copy.wait()
    grad = lax.dot_general(
        down, cotangent_v[...], (((0,), (0,)), ((), ())), preferred_element_type=F32
    )
    for k in range(ctx_count):
        partial[k] = grad[k * own_rank:(k + 1) * own_rank]

    pl.semaphore_wait(barrier, ctx_count - 1 + slots - 1)

    def grad_copy(d, landing=None):
        other = ctx_peer(d)
        source = ctx if landing is None else other
        return pltpu.make_async_remote_copy(
            src_ref=partial.at[other], dst_ref=partial_in.at[source],
            send_sem=grad_send.at[d], recv_sem=grad_recv.at[source],
            device_id={"ctx": other}, device_id_type=MESH,
        )

    def ids_copy(d, landing=None):
        other = lax.rem(group + d, group_count)
        source = group if landing is None else other
        return pltpu.make_async_remote_copy(
            src_ref=ids.at[source], dst_ref=ids.at[source],
            send_sem=ids_send.at[d], recv_sem=ids_recv.at[source],
            device_id={"group": other}, device_id_type=MESH,
        )

    loop(1, ctx_count, lambda d: grad_copy(d).start())
    loop(1, group_count, lambda d: ids_copy(d).start())
    partial_in[ctx] = partial[ctx]

    loop(1, group_count, lambda d: ids_copy(d, True).wait_recv())
    pick_shape = (own_rank * pieces * padded, slots * block)
    row = lax.broadcasted_iota(jnp.int32, pick_shape, 0)
    column = lax.broadcasted_iota(jnp.int32, pick_shape, 1)
    column_id = jnp.zeros(pick_shape, jnp.int32)
    for f in range(feat_count):
        for x in range(side_count):
            i = f * ex_count + x % ex_count
            value = ids[x // ex_count, :1, i:i + 1] + (x // ex_count) * group_slots
            column_id = jnp.where(column // block == f * side_count + x, value, column_id)
    wanted = lax.rem(row // padded, pieces) * own_rank + row // (padded * pieces)
    pick = (lax.rem(column, block) == wanted) & (lax.rem(row, padded) == column_id)
    pick = pick.astype(F32).astype(BF16)

    loop(1, ctx_count, lambda d: grad_copy(d, True).wait_recv())
    total = partial_in[0]
    for k in range(1, ctx_count):
        total += partial_in[k]
    rows = [total[:, q * block_lanes:(q + 1) * block_lanes] for q in range(pieces)]
    if pieces * own_rank < block:
        rows.append(jnp.zeros((block - pieces * own_rank, block_lanes), F32))
    grads[slot] = jnp.concatenate(rows, axis=0).astype(BF16)

    def gather_copy(d, landing=None):
        other, device = slot_peer(d)
        source = slot if landing is None else other
        return pltpu.make_async_remote_copy(
            src_ref=grads.at[source], dst_ref=grads.at[source],
            send_sem=gather_send.at[d], recv_sem=gather_recv.at[source],
            device_id=device, device_id_type=MESH,
        )

    loop(1, slots, lambda d: gather_copy(d).start())
    loop(1, slots, lambda d: gather_copy(d, True).wait_recv())
    gathered = grads[...].reshape(slots * block, block_lanes)
    picked = jnp.dot(pick, gathered, preferred_element_type=F32)
    left = [picked[i * padded:(i + 1) * padded].astype(BF16) for i in range(own_rank * pieces)]

    def rows_copy(h, d, landing=None):
        other = ctx_peer(d)
        source = ctx if landing is None else other
        return pltpu.make_async_remote_copy(
            src_ref=rows_out.at[h], dst_ref=rows_in.at[source, h],
            send_sem=rows_send.at[h, d], recv_sem=rows_recv.at[h, source],
            device_id={"ctx": other}, device_id_type=MESH,
        )

    def project(k, carry):
        projection_copy(k).wait()
        product = jnp.zeros((padded, chunk), F32)
        for i in range(own_rank * pieces):
            product += jnp.dot(
                left[i], projection_v[k, i * block_lanes:(i + 1) * block_lanes, :],
                preferred_element_type=F32,
            )
        lanes = [product[:slots, p * LANES:(p + 1) * LANES] for p in range(chunk // LANES)]
        rows_out[k] = jnp.concatenate(lanes, axis=0).astype(BF16)
        for d in range(1, ctx_count):
            rows_copy(k, d).start()
        rows_in[ctx, k] = rows_out[k]
        return carry

    lax.fori_loop(0, chunk_count, project, 0)

    for k in range(chunk_count):
        loop(1, ctx_count, lambda d: rows_copy(k, d, True).wait_recv())
        summed = rows_in[0, k].astype(F32)
        for c in range(1, ctx_count):
            summed += rows_in[c, k].astype(F32)
        lanes = [summed[p * slots:(p + 1) * slots] for p in range(chunk // LANES)]
        square = lanes[0] * lanes[0]
        for part in lanes[1:]:
            square += part * part
        square = jnp.broadcast_to(jnp.sum(square, axis=1, keepdims=True), (slots, LANES))
        there = slice(k * own_ids, (k + 1) * own_ids)
        for x in range(side_count):
            here = slice(x * own_ids, (x + 1) * own_ids)
            for p, part in enumerate(lanes + [square]):
                final_out[x, there, p * LANES:(p + 1) * LANES] = part[here]

    tail = pl.ds(chunk, LANES)

    def final_copy(d, landing=None):
        other = lax.rem(side + d, side_count)
        source = side if landing is None else other
        return pltpu.make_async_remote_copy(
            src_ref=final_out.at[other], dst_ref=final_in.at[source],
            send_sem=final_send.at[d], recv_sem=final_recv.at[source],
            device_id=at_side(other), device_id_type=MESH,
        )

    def squares_copy(q, landing=None):
        g, x = q // side_count + 1, lax.rem(side + lax.rem(q, side_count), side_count)
        other = lax.rem(feat + g, feat_count)
        source = slot if landing is None else other * side_count + x
        return pltpu.make_async_remote_copy(
            src_ref=final_out.at[x, :, tail], dst_ref=squares_in.at[source],
            send_sem=squares_send.at[q], recv_sem=squares_recv.at[source],
            device_id={"feat": other, **at_side(x)}, device_id_type=MESH,
        )

    square_sends = (feat_count - 1) * side_count
    loop(0, square_sends, lambda q: squares_copy(q).start())
    loop(1, side_count, lambda d: final_copy(d).start())
    final_in[side] = final_out[side]
    loop(1, side_count, lambda d: final_copy(d, True).wait_recv())
    for x in range(side_count):
        squares_in[feat * side_count + x] = final_in[x, :, chunk:]
    loop(0, square_sends, lambda q: squares_copy(q, True).wait_recv())
    everything = squares_in[0]
    for s in range(1, slots):
        everything += squares_in[s]
    norm = everything[:own_ids, :1]
    for k in range(1, chunk_count):
        norm += everything[k * own_ids:(k + 1) * own_ids, :1]
    norm = jnp.sqrt(norm / (feat_count * side_count * width) + 1e-06)
    for x in range(side_count):
        for k in range(chunk_count):
            place = x * width + k * chunk
            out_ref[:, place:place + chunk] = final_in[x, k * own_ids:(k + 1) * own_ids, :chunk] / norm

    loop(1, ctx_count, lambda d: grad_copy(d).wait_send())
    loop(1, slots, lambda d: gather_copy(d).wait_send())
    for k in range(chunk_count):
        loop(1, ctx_count, lambda d: rows_copy(k, d).wait_send())
    loop(1, group_count, lambda d: ids_copy(d).wait_send())
    loop(1, side_count, lambda d: final_copy(d).wait_send())
    loop(0, square_sends, lambda q: squares_copy(q).wait_send())


def per_device(sizes, hidden, cotangent, adapter_down_factor, projection, lengths, slot_example_order):
    group_count, ctx_count, feat_count, ex_count = sizes
    side_count = group_count * ex_count
    slots = feat_count * side_count
    example_count, token_count, model_width = hidden.shape
    value_width = cotangent.shape[2]
    rank = adapter_down_factor.shape[1]
    depth, columns = projection.shape
    width = columns // side_count
    chunk = min(256, width)
    chunk_count = width // chunk
    own_ids = slots // side_count
    own_rank = rank // ctx_count
    block_lanes = max(LANES, own_rank * value_width // 16)
    block = -(-own_rank * value_width // block_lanes // 16) * 16
    assert example_count == 1 and depth == own_rank * value_width
    dma = pltpu.SemaphoreType.DMA
    return pl.pallas_call(
        functools.partial(kernel, sizes),
        out_shape=jax.ShapeDtypeStruct((own_ids, columns), F32),
        in_specs=[pl.BlockSpec(memory_space=pltpu.HBM)] * 6,
        out_specs=pl.BlockSpec(memory_space=pltpu.VMEM),
        scratch_shapes=[
            pltpu.SMEM(lengths.shape, jnp.int32),
            pltpu.SMEM(slot_example_order.shape, jnp.int32),
            pltpu.VMEM((token_count, model_width), BF16),
            pltpu.VMEM((token_count, value_width), BF16),
            pltpu.VMEM((rank, model_width), BF16),
            pltpu.VMEM((chunk_count, depth, chunk), BF16),
            pltpu.VMEM((group_count, 8, LANES), jnp.int32),
            pltpu.VMEM((ctx_count, own_rank, value_width), F32),
            pltpu.VMEM((ctx_count, own_rank, value_width), F32),
            pltpu.VMEM((slots, block, block_lanes), BF16),
            pltpu.VMEM((chunk_count, slots * chunk // LANES, LANES), BF16),
            pltpu.VMEM((ctx_count, chunk_count, slots * chunk // LANES, LANES), BF16),
            pltpu.VMEM((side_count, chunk_count * own_ids, chunk + LANES), F32),
            pltpu.VMEM((side_count, chunk_count * own_ids, chunk + LANES), F32),
            pltpu.VMEM((slots, chunk_count * own_ids, LANES), F32),
            dma((4 + HIDDEN_CHUNKS,)),
            dma((chunk_count,)),
            dma((group_count,)),
            dma((group_count,)),
            dma((ctx_count,)),
            dma((ctx_count,)),
            dma((slots,)),
            dma((slots,)),
            dma((chunk_count, ctx_count)),
            dma((chunk_count, ctx_count)),
            dma((side_count,)),
            dma((side_count,)),
            dma(((feat_count - 1) * side_count,)),
            dma((slots,)),
        ],
        compiler_params=pltpu.CompilerParams(
            collective_id=0, has_side_effects=True, vmem_limit_bytes=215 * 1024 * 256
        ),
    )(lengths, slot_example_order, hidden, cotangent, adapter_down_factor.T, projection)


def solution(mesh):
    in_specs = (
        P(("group", "feat", "ex"), "ctx", None),
        P(("group", "feat", "ex"), "ctx", None),
        P(),
        P("ctx", "feat"),
        P(("group", "feat", "ex")),
        P("group"),
    )
    out_specs = P(("group", "ex"), "feat")
    sizes = (mesh.shape["group"], mesh.shape["ctx"], mesh.shape["feat"], mesh.shape["ex"])
    return jax.shard_map(
        functools.partial(per_device, sizes),
        mesh=mesh, in_specs=in_specs, out_specs=out_specs, check_vma=False,
    )
```

```python
import functools

import jax
import jax.numpy as jnp
from jax import lax
from jax.experimental import pallas as pl
from jax.experimental.pallas import tpu as pltpu
from jax.sharding import PartitionSpec as P

MESH = pl.DeviceIdType.MESH
F32 = jnp.float32
BF16 = jnp.bfloat16
LANES = 128
HIDDEN_CHUNKS = 4


def loop(low, high, body):
    if high - low <= 8:
        for step in range(low, high):
            body(step)
    else:
        lax.fori_loop(low, high, lambda step, carry: (body(step), carry)[1], 0)


def kernel(
    sizes,
    numbers_ref, hidden_ref, cotangent_ref, factor_ref, projection_ref,
    out_ref,
    numbers_v, hidden_v, cotangent_v, factor_v, projection_v,
    ids, partial, partial_in, grads, rows_out, rows_in, final_out, final_in, squares_in,
    local_sem, projection_sem, ids_send, ids_recv,
    grad_send, grad_recv, gather_send, gather_recv, rows_send, rows_recv,
    final_send, final_recv, squares_send, squares_recv,
):
    group_count, ctx_count, feat_count, ex_count = sizes
    group, ctx, feat = lax.axis_index("group"), lax.axis_index("ctx"), lax.axis_index("feat")
    ex = lax.axis_index("ex")
    side_count = group_count * ex_count
    side = group * ex_count + ex
    slots = feat_count * side_count
    slot = feat * side_count + side
    group_slots = feat_count * ex_count
    token_count, model_width = hidden_v.shape
    rank = factor_v.shape[0]
    own_rank = rank // ctx_count
    chunk_count, depth, chunk = projection_v.shape
    width = chunk_count * chunk
    value_width = cotangent_v.shape[1]
    padded = max(8, slots)
    own_ids = out_ref.shape[0]
    block, block_lanes = grads.shape[1:]
    pieces = value_width // block_lanes

    step = model_width // HIDDEN_CHUNKS
    factor_copy = pltpu.make_async_copy(factor_ref, factor_v, local_sem.at[0])
    factor_copy.start()

    def hidden_copy(k):
        columns = pl.ds(pl.multiple_of(k * step, LANES), step)
        return pltpu.make_async_copy(
            hidden_ref.at[0, :, columns], hidden_v.at[:, columns], local_sem.at[4 + k]
        )

    for k in range(HIDDEN_CHUNKS):
        hidden_copy(k).start()
    numbers_copy = pltpu.make_async_copy(numbers_ref, numbers_v, local_sem.at[2])
    numbers_copy.start()
    cotangent_copy = pltpu.make_async_copy(cotangent_ref.at[0], cotangent_v, local_sem.at[1])
    cotangent_copy.start()

    def projection_copy(k):
        columns = pl.ds(pl.multiple_of(side * width + k * chunk, LANES), chunk)
        return pltpu.make_async_copy(
            projection_ref.at[:, columns], projection_v.at[k], projection_sem.at[k]
        )

    def at_side(x):
        return {"group": x // ex_count, "ex": lax.rem(x, ex_count)}

    def ctx_peer(d):
        return lax.rem(ctx + d, ctx_count)

    def slot_peer(d):
        other = lax.rem(slot + d, slots)
        return other, {"feat": other // side_count, **at_side(lax.rem(other, side_count))}

    barrier = pltpu.get_barrier_semaphore()

    def greet_ctx(d):
        pl.semaphore_signal(
            barrier, inc=1, device_id_type=MESH, device_id={"ctx": ctx_peer(d)}
        )

    def greet_slot(d):
        pl.semaphore_signal(
            barrier, inc=1, device_id_type=MESH, device_id=slot_peer(d)[1]
        )

    loop(1, ctx_count, greet_ctx)
    loop(1, slots, greet_slot)

    numbers_copy.wait()
    lane = lax.broadcasted_iota(jnp.int32, ids.shape[1:], 1)
    own_order = jnp.zeros(ids.shape[1:], jnp.int32)
    for i in range(group_slots):
        own_order = jnp.where(lane == i, numbers_v[1 + i], own_order)
    ids[group] = own_order

    factor_copy.wait()
    def add_down(k, down):
        hidden_copy(k).wait()

        @pl.when(k == HIDDEN_CHUNKS - 1)
        def _():
            for j in range(chunk_count):
                projection_copy(j).start()

        columns = pl.ds(pl.multiple_of(k * step, LANES), step)
        return down + lax.dot_general(
            factor_v[:, columns], hidden_v[:, columns], (((1,), (1,)), ((), ())),
            preferred_element_type=F32,
        )

    down = lax.fori_loop(0, HIDDEN_CHUNKS, add_down, jnp.zeros((rank, token_count), F32))
    position = ctx * token_count + lax.broadcasted_iota(jnp.int32, down.shape, 1)
    down = jnp.where(position < numbers_v[0], down, 0.0).astype(BF16)
    cotangent_copy.wait()
    grad = jnp.dot(down, cotangent_v[...], preferred_element_type=F32)
    for k in range(ctx_count):
        partial[k] = grad[k * own_rank:(k + 1) * own_rank]

    pl.semaphore_wait(barrier, ctx_count - 1 + slots - 1)

    def grad_copy(d, landing=None):
        other = ctx_peer(d)
        source = ctx if landing is None else other
        return pltpu.make_async_remote_copy(
            src_ref=partial.at[other], dst_ref=partial_in.at[source],
            send_sem=grad_send.at[d], recv_sem=grad_recv.at[source],
            device_id={"ctx": other}, device_id_type=MESH,
        )

    def ids_copy(d, landing=None):
        other = lax.rem(group + d, group_count)
        source = group if landing is None else other
        return pltpu.make_async_remote_copy(
            src_ref=ids.at[source], dst_ref=ids.at[source],
            send_sem=ids_send.at[d], recv_sem=ids_recv.at[source],
            device_id={"group": other}, device_id_type=MESH,
        )

    loop(1, ctx_count, lambda d: grad_copy(d).start())
    loop(1, group_count, lambda d: ids_copy(d).start())
    partial_in[ctx] = partial[ctx]

    loop(1, group_count, lambda d: ids_copy(d, True).wait_recv())
    pick_shape = (own_rank * pieces * padded, slots * block)
    row = lax.broadcasted_iota(jnp.int32, pick_shape, 0)
    column = lax.broadcasted_iota(jnp.int32, pick_shape, 1)
    column_id = jnp.zeros(pick_shape, jnp.int32)
    for f in range(feat_count):
        for x in range(side_count):
            i = f * ex_count + x % ex_count
            value = ids[x // ex_count, :1, i:i + 1] + (x // ex_count) * group_slots
            column_id = jnp.where(column // block == f * side_count + x, value, column_id)
    wanted = lax.rem(row // padded, pieces) * own_rank + row // (padded * pieces)
    pick = (lax.rem(column, block) == wanted) & (lax.rem(row, padded) == column_id)
    pick = pick.astype(F32).astype(BF16)

    loop(1, ctx_count, lambda d: grad_copy(d, True).wait_recv())
    total = partial_in[0]
    for k in range(1, ctx_count):
        total += partial_in[k]
    rows = [total[:, q * block_lanes:(q + 1) * block_lanes] for q in range(pieces)]
    if pieces * own_rank < block:
        rows.append(jnp.zeros((block - pieces * own_rank, block_lanes), F32))
    grads[slot] = jnp.concatenate(rows, axis=0).astype(BF16)

    def gather_copy(d, landing=None):
        other, device = slot_peer(d)
        source = slot if landing is None else other
        return pltpu.make_async_remote_copy(
            src_ref=grads.at[source], dst_ref=grads.at[source],
            send_sem=gather_send.at[d], recv_sem=gather_recv.at[source],
            device_id=device, device_id_type=MESH,
        )

    loop(1, slots, lambda d: gather_copy(d).start())
    loop(1, slots, lambda d: gather_copy(d, True).wait_recv())
    gathered = grads[...].reshape(slots * block, block_lanes)
    picked = jnp.dot(pick, gathered, preferred_element_type=F32)
    left = [picked[i * padded:(i + 1) * padded].astype(BF16) for i in range(own_rank * pieces)]

    def rows_copy(h, d, landing=None):
        other = ctx_peer(d)
        source = ctx if landing is None else other
        return pltpu.make_async_remote_copy(
            src_ref=rows_out.at[h], dst_ref=rows_in.at[source, h],
            send_sem=rows_send.at[h, d], recv_sem=rows_recv.at[h, source],
            device_id={"ctx": other}, device_id_type=MESH,
        )

    def project(k, carry):
        projection_copy(k).wait()
        product = jnp.zeros((padded, chunk), F32)
        for i in range(own_rank * pieces):
            product += jnp.dot(
                left[i], projection_v[k, i * block_lanes:(i + 1) * block_lanes, :],
                preferred_element_type=F32,
            )
        lanes = [product[:slots, p * LANES:(p + 1) * LANES] for p in range(chunk // LANES)]
        rows_out[k] = jnp.concatenate(lanes, axis=0).astype(BF16)
        for d in range(1, ctx_count):
            rows_copy(k, d).start()
        rows_in[ctx, k] = rows_out[k]
        return carry

    lax.fori_loop(0, chunk_count, project, 0)

    for k in range(chunk_count):
        loop(1, ctx_count, lambda d: rows_copy(k, d, True).wait_recv())
        summed = rows_in[0, k].astype(F32)
        for c in range(1, ctx_count):
            summed += rows_in[c, k].astype(F32)
        lanes = [summed[p * slots:(p + 1) * slots] for p in range(chunk // LANES)]
        square = lanes[0] * lanes[0]
        for part in lanes[1:]:
            square += part * part
        square = jnp.broadcast_to(jnp.sum(square, axis=1, keepdims=True), (slots, LANES))
        there = slice(k * own_ids, (k + 1) * own_ids)
        for x in range(side_count):
            here = slice(x * own_ids, (x + 1) * own_ids)
            for p, part in enumerate(lanes + [square]):
                final_out[x, there, p * LANES:(p + 1) * LANES] = part[here]

    tail = pl.ds(chunk, LANES)

    def final_copy(d, landing=None):
        other = lax.rem(side + d, side_count)
        source = side if landing is None else other
        return pltpu.make_async_remote_copy(
            src_ref=final_out.at[other], dst_ref=final_in.at[source],
            send_sem=final_send.at[d], recv_sem=final_recv.at[source],
            device_id=at_side(other), device_id_type=MESH,
        )

    def squares_copy(q, landing=None):
        g, x = q // side_count + 1, lax.rem(side + lax.rem(q, side_count), side_count)
        other = lax.rem(feat + g, feat_count)
        source = slot if landing is None else other * side_count + x
        return pltpu.make_async_remote_copy(
            src_ref=final_out.at[x, :, tail], dst_ref=squares_in.at[source],
            send_sem=squares_send.at[q], recv_sem=squares_recv.at[source],
            device_id={"feat": other, **at_side(x)}, device_id_type=MESH,
        )

    square_sends = (feat_count - 1) * side_count
    loop(1, side_count, lambda d: final_copy(d).start())
    loop(0, square_sends, lambda q: squares_copy(q).start())
    final_in[side] = final_out[side]
    loop(1, side_count, lambda d: final_copy(d, True).wait_recv())
    for x in range(side_count):
        squares_in[feat * side_count + x] = final_in[x, :, chunk:]
    loop(0, square_sends, lambda q: squares_copy(q, True).wait_recv())
    everything = squares_in[0]
    for s in range(1, slots):
        everything += squares_in[s]
    norm = everything[:own_ids, :1]
    for k in range(1, chunk_count):
        norm += everything[k * own_ids:(k + 1) * own_ids, :1]
    norm = jnp.sqrt(norm / (feat_count * side_count * width) + 1e-06)
    for x in range(side_count):
        for k in range(chunk_count):
            place = x * width + k * chunk
            out_ref[:, place:place + chunk] = final_in[x, k * own_ids:(k + 1) * own_ids, :chunk] / norm

    loop(1, ctx_count, lambda d: grad_copy(d).wait_send())
    loop(1, slots, lambda d: gather_copy(d).wait_send())
    for k in range(chunk_count):
        loop(1, ctx_count, lambda d: rows_copy(k, d).wait_send())
    loop(1, group_count, lambda d: ids_copy(d).wait_send())
    loop(1, side_count, lambda d: final_copy(d).wait_send())
    loop(0, square_sends, lambda q: squares_copy(q).wait_send())


def per_device(sizes, hidden, cotangent, adapter_down_factor, projection, lengths, slot_example_order):
    group_count, ctx_count, feat_count, ex_count = sizes
    side_count = group_count * ex_count
    slots = feat_count * side_count
    example_count, token_count, model_width = hidden.shape
    value_width = cotangent.shape[2]
    rank = adapter_down_factor.shape[1]
    depth, columns = projection.shape
    width = columns // side_count
    chunk = min(256, width)
    chunk_count = width // chunk
    own_ids = slots // side_count
    own_rank = rank // ctx_count
    block_lanes = max(LANES, own_rank * value_width // 16)
    block = -(-own_rank * value_width // block_lanes // 16) * 16
    assert example_count == 1 and depth == own_rank * value_width
    numbers = jnp.concatenate([lengths, slot_example_order])
    dma = pltpu.SemaphoreType.DMA
    return pl.pallas_call(
        functools.partial(kernel, sizes),
        out_shape=jax.ShapeDtypeStruct((own_ids, columns), F32),
        in_specs=[pl.BlockSpec(memory_space=pltpu.HBM)] * 5,
        out_specs=pl.BlockSpec(memory_space=pltpu.VMEM),
        scratch_shapes=[
            pltpu.SMEM(numbers.shape, jnp.int32),
            pltpu.VMEM((token_count, model_width), BF16),
            pltpu.VMEM((token_count, value_width), BF16),
            pltpu.VMEM((rank, model_width), BF16),
            pltpu.VMEM((chunk_count, depth, chunk), BF16),
            pltpu.VMEM((group_count, 8, LANES), jnp.int32),
            pltpu.VMEM((ctx_count, own_rank, value_width), F32),
            pltpu.VMEM((ctx_count, own_rank, value_width), F32),
            pltpu.VMEM((slots, block, block_lanes), BF16),
            pltpu.VMEM((chunk_count, slots * chunk // LANES, LANES), BF16),
            pltpu.VMEM((ctx_count, chunk_count, slots * chunk // LANES, LANES), BF16),
            pltpu.VMEM((side_count, chunk_count * own_ids, chunk + LANES), F32),
            pltpu.VMEM((side_count, chunk_count * own_ids, chunk + LANES), F32),
            pltpu.VMEM((slots, chunk_count * own_ids, LANES), F32),
            dma((4 + HIDDEN_CHUNKS,)),
            dma((chunk_count,)),
            dma((group_count,)),
            dma((group_count,)),
            dma((ctx_count,)),
            dma((ctx_count,)),
            dma((slots,)),
            dma((slots,)),
            dma((chunk_count, ctx_count)),
            dma((chunk_count, ctx_count)),
            dma((side_count,)),
            dma((side_count,)),
            dma(((feat_count - 1) * side_count,)),
            dma((slots,)),
        ],
        compiler_params=pltpu.CompilerParams(
            collective_id=0, has_side_effects=True, vmem_limit_bytes=215 * 1024 * 256
        ),
    )(numbers, hidden, cotangent, adapter_down_factor.T, projection)


def solution(mesh):
    in_specs = (
        P(("group", "feat", "ex"), "ctx", None),
        P(("group", "feat", "ex"), "ctx", None),
        P(),
        P("ctx", "feat"),
        P(("group", "feat", "ex")),
        P("group"),
    )
    out_specs = P(("group", "ex"), "feat")
    sizes = (mesh.shape["group"], mesh.shape["ctx"], mesh.shape["feat"], mesh.shape["ex"])
    return jax.shard_map(
        functools.partial(per_device, sizes),
        mesh=mesh, in_specs=in_specs, out_specs=out_specs, check_vma=False,
    )
```

```python
import functools

import jax
import jax.numpy as jnp
from jax import lax
from jax.experimental import pallas as pl
from jax.experimental.pallas import tpu as pltpu
from jax.sharding import PartitionSpec as P

MESH = pl.DeviceIdType.MESH
F32 = jnp.float32
BF16 = jnp.bfloat16
LANES = 128
HIDDEN_CHUNKS = 4


def loop(low, high, body):
    if high - low <= 8:
        for step in range(low, high):
            body(step)
    else:
        lax.fori_loop(low, high, lambda step, carry: (body(step), carry)[1], 0)


def kernel(
    sizes,
    lengths_ref, order_ref, hidden_ref, cotangent_ref, factor_ref, projection_ref,
    out_ref,
    lengths_v, order_v, hidden_v, cotangent_v, factor_v, projection_v,
    ids, own_partial, partial, partial_in, grads, rows_out, rows_in, final_out, final_in, squares_in,
    local_sem, projection_sem, ids_send, ids_recv,
    grad_send, grad_recv, gather_send, gather_recv, rows_send, rows_recv,
    final_send, final_recv, squares_send, squares_recv,
):
    group_count, ctx_count, feat_count, ex_count = sizes
    group, ctx, feat = lax.axis_index("group"), lax.axis_index("ctx"), lax.axis_index("feat")
    ex = lax.axis_index("ex")
    side_count = group_count * ex_count
    side = group * ex_count + ex
    slots = feat_count * side_count
    slot = feat * side_count + side
    group_slots = feat_count * ex_count
    token_count, model_width = hidden_v.shape
    rank = factor_v.shape[0]
    own_rank = rank // ctx_count
    chunk_count, depth, chunk = projection_v.shape
    width = chunk_count * chunk
    value_width = cotangent_v.shape[1]
    padded = max(8, slots)
    own_ids = out_ref.shape[0]
    block, block_lanes = grads.shape[1:]
    pieces = value_width // block_lanes

    step = model_width // HIDDEN_CHUNKS
    factor_copy = pltpu.make_async_copy(factor_ref, factor_v, local_sem.at[0])
    factor_copy.start()

    def hidden_copy(k):
        columns = pl.ds(pl.multiple_of(k * step, LANES), step)
        return pltpu.make_async_copy(
            hidden_ref.at[0, :, columns], hidden_v.at[:, columns], local_sem.at[4 + k]
        )

    for k in range(HIDDEN_CHUNKS):
        hidden_copy(k).start()
    order_copy = pltpu.make_async_copy(order_ref, order_v, local_sem.at[2])
    order_copy.start()
    lengths_copy = pltpu.make_async_copy(lengths_ref, lengths_v, local_sem.at[3])
    lengths_copy.start()
    cotangent_copy = pltpu.make_async_copy(cotangent_ref.at[0], cotangent_v, local_sem.at[1])
    cotangent_copy.start()

    def projection_copy(k):
        columns = pl.ds(pl.multiple_of(side * width + k * chunk, LANES), chunk)
        return pltpu.make_async_copy(
            projection_ref.at[:, columns], projection_v.at[k], projection_sem.at[k]
        )

    def at_side(x):
        return {"group": x // ex_count, "ex": lax.rem(x, ex_count)}

    def ctx_peer(d):
        return lax.rem(ctx + d, ctx_count)

    def slot_peer(d):
        other = lax.rem(slot + d, slots)
        return other, {"feat": other // side_count, **at_side(lax.rem(other, side_count))}

    barrier = pltpu.get_barrier_semaphore()

    def greet_ctx(d):
        pl.semaphore_signal(
            barrier, inc=1, device_id_type=MESH, device_id={"ctx": ctx_peer(d)}
        )

    def greet_slot(d):
        pl.semaphore_signal(
            barrier, inc=1, device_id_type=MESH, device_id=slot_peer(d)[1]
        )

    loop(1, ctx_count, greet_ctx)
    loop(1, slots, greet_slot)

    order_copy.wait()
    lane = lax.broadcasted_iota(jnp.int32, ids.shape[1:], 1)
    own_order = jnp.zeros(ids.shape[1:], jnp.int32)
    for i in range(group_slots):
        own_order = jnp.where(lane == i, order_v[i], own_order)
    ids[group] = own_order

    lengths_copy.wait()
    factor_copy.wait()
    hidden_copy(0).wait()
    for k in range(chunk_count):
        projection_copy(k).start()

    def add_down(k, down):
        @pl.when(k > 0)
        def _():
            hidden_copy(k).wait()

        columns = pl.ds(pl.multiple_of(k * step, LANES), step)
        return down + lax.dot_general(
            factor_v[:, columns], hidden_v[:, columns], (((1,), (1,)), ((), ())),
            preferred_element_type=F32,
        )

    down = lax.fori_loop(0, HIDDEN_CHUNKS, add_down, jnp.zeros((rank, token_count), F32))
    position = ctx * token_count + lax.broadcasted_iota(jnp.int32, down.shape, 1)
    down = jnp.where(position < lengths_v[0], down, 0.0).astype(BF16)
    cotangent_copy.wait()
    grad = jnp.dot(down, cotangent_v[...], preferred_element_type=F32)
    for k in range(ctx_count):
        rows = [
            grad[k * own_rank:(k + 1) * own_rank, q * block_lanes:(q + 1) * block_lanes]
            for q in range(pieces)
        ]
        if pieces * own_rank < block:
            rows.append(jnp.zeros((block - pieces * own_rank, block_lanes), F32))
        own_partial[k] = jnp.concatenate(rows, axis=0)
        partial[k] = own_partial[k].astype(BF16)

    pl.semaphore_wait(barrier, ctx_count - 1 + slots - 1)

    def grad_copy(d, landing=None):
        other = ctx_peer(d)
        source = ctx if landing is None else other
        return pltpu.make_async_remote_copy(
            src_ref=partial.at[other], dst_ref=partial_in.at[source],
            send_sem=grad_send.at[d], recv_sem=grad_recv.at[source],
            device_id={"ctx": other}, device_id_type=MESH,
        )

    def ids_copy(d, landing=None):
        other = lax.rem(group + d, group_count)
        source = group if landing is None else other
        return pltpu.make_async_remote_copy(
            src_ref=ids.at[source], dst_ref=ids.at[source],
            send_sem=ids_send.at[d], recv_sem=ids_recv.at[source],
            device_id={"group": other}, device_id_type=MESH,
        )

    loop(1, ctx_count, lambda d: grad_copy(d).start())
    loop(1, group_count, lambda d: ids_copy(d).start())

    loop(1, group_count, lambda d: ids_copy(d, True).wait_recv())
    pick_shape = (own_rank * pieces * padded, slots * block)
    row = lax.broadcasted_iota(jnp.int32, pick_shape, 0)
    column = lax.broadcasted_iota(jnp.int32, pick_shape, 1)
    column_id = jnp.zeros(pick_shape, jnp.int32)
    for f in range(feat_count):
        for x in range(side_count):
            i = f * ex_count + x % ex_count
            value = ids[x // ex_count, :1, i:i + 1] + (x // ex_count) * group_slots
            column_id = jnp.where(column // block == f * side_count + x, value, column_id)
    wanted = lax.rem(row // padded, pieces) * own_rank + row // (padded * pieces)
    pick = (lax.rem(column, block) == wanted) & (lax.rem(row, padded) == column_id)
    pick = pick.astype(F32).astype(BF16)

    loop(1, ctx_count, lambda d: grad_copy(d, True).wait_recv())
    total = own_partial[ctx]
    for d in range(1, ctx_count):
        total += partial_in[ctx_peer(d)].astype(F32)
    grads[slot] = total.astype(BF16)

    def gather_copy(d, landing=None):
        other, device = slot_peer(d)
        source = slot if landing is None else other
        return pltpu.make_async_remote_copy(
            src_ref=grads.at[source], dst_ref=grads.at[source],
            send_sem=gather_send.at[d], recv_sem=gather_recv.at[source],
            device_id=device, device_id_type=MESH,
        )

    loop(1, slots, lambda d: gather_copy(d).start())
    loop(1, slots, lambda d: gather_copy(d, True).wait_recv())
    gathered = grads[...].reshape(slots * block, block_lanes)
    picked = jnp.dot(pick, gathered, preferred_element_type=F32)
    left = [picked[i * padded:(i + 1) * padded].astype(BF16) for i in range(own_rank * pieces)]

    def rows_copy(h, d, landing=None):
        other = ctx_peer(d)
        source = ctx if landing is None else other
        return pltpu.make_async_remote_copy(
            src_ref=rows_out.at[h], dst_ref=rows_in.at[source, h],
            send_sem=rows_send.at[h, d], recv_sem=rows_recv.at[h, source],
            device_id={"ctx": other}, device_id_type=MESH,
        )

    def project(k, carry):
        projection_copy(k).wait()
        product = jnp.zeros((padded, chunk), F32)
        for i in range(own_rank * pieces):
            product += jnp.dot(
                left[i], projection_v[k, i * block_lanes:(i + 1) * block_lanes, :],
                preferred_element_type=F32,
            )
        lanes = [product[:slots, p * LANES:(p + 1) * LANES] for p in range(chunk // LANES)]
        rows_out[k] = jnp.concatenate(lanes, axis=0).astype(BF16)
        for d in range(1, ctx_count):
            rows_copy(k, d).start()
        rows_in[ctx, k] = rows_out[k]
        return carry

    lax.fori_loop(0, chunk_count, project, 0)

    for k in range(chunk_count):
        loop(1, ctx_count, lambda d: rows_copy(k, d, True).wait_recv())
        summed = rows_in[0, k].astype(F32)
        for c in range(1, ctx_count):
            summed += rows_in[c, k].astype(F32)
        lanes = [summed[p * slots:(p + 1) * slots] for p in range(chunk // LANES)]
        square = lanes[0] * lanes[0]
        for part in lanes[1:]:
            square += part * part
        square = jnp.broadcast_to(jnp.sum(square, axis=1, keepdims=True), (slots, LANES))
        there = slice(k * own_ids, (k + 1) * own_ids)
        for x in range(side_count):
            here = slice(x * own_ids, (x + 1) * own_ids)
            for p, part in enumerate(lanes + [square]):
                final_out[x, there, p * LANES:(p + 1) * LANES] = part[here]

    tail = pl.ds(chunk, LANES)

    def final_copy(d, landing=None):
        other = lax.rem(side + d, side_count)
        source = side if landing is None else other
        return pltpu.make_async_remote_copy(
            src_ref=final_out.at[other], dst_ref=final_in.at[source],
            send_sem=final_send.at[d], recv_sem=final_recv.at[source],
            device_id=at_side(other), device_id_type=MESH,
        )

    def squares_copy(q, landing=None):
        g, x = q // side_count + 1, lax.rem(side + lax.rem(q, side_count), side_count)
        other = lax.rem(feat + g, feat_count)
        source = slot if landing is None else other * side_count + x
        return pltpu.make_async_remote_copy(
            src_ref=final_out.at[x, :, tail], dst_ref=squares_in.at[source],
            send_sem=squares_send.at[q], recv_sem=squares_recv.at[source],
            device_id={"feat": other, **at_side(x)}, device_id_type=MESH,
        )

    square_sends = (feat_count - 1) * side_count
    loop(1, side_count, lambda d: final_copy(d).start())
    loop(0, square_sends, lambda q: squares_copy(q).start())
    final_in[side] = final_out[side]
    loop(1, side_count, lambda d: final_copy(d, True).wait_recv())
    for x in range(side_count):
        squares_in[feat * side_count + x] = final_in[x, :, chunk:]
    loop(0, square_sends, lambda q: squares_copy(q, True).wait_recv())
    everything = squares_in[0]
    for s in range(1, slots):
        everything += squares_in[s]
    norm = everything[:own_ids, :1]
    for k in range(1, chunk_count):
        norm += everything[k * own_ids:(k + 1) * own_ids, :1]
    norm = jnp.sqrt(norm / (feat_count * side_count * width) + 1e-06)
    for x in range(side_count):
        for k in range(chunk_count):
            place = x * width + k * chunk
            out_ref[:, place:place + chunk] = final_in[x, k * own_ids:(k + 1) * own_ids, :chunk] / norm

    loop(1, ctx_count, lambda d: grad_copy(d).wait_send())
    loop(1, slots, lambda d: gather_copy(d).wait_send())
    for k in range(chunk_count):
        loop(1, ctx_count, lambda d: rows_copy(k, d).wait_send())
    loop(1, group_count, lambda d: ids_copy(d).wait_send())
    loop(1, side_count, lambda d: final_copy(d).wait_send())
    loop(0, square_sends, lambda q: squares_copy(q).wait_send())


def per_device(sizes, hidden, cotangent, adapter_down_factor, projection, lengths, slot_example_order):
    group_count, ctx_count, feat_count, ex_count = sizes
    side_count = group_count * ex_count
    slots = feat_count * side_count
    example_count, token_count, model_width = hidden.shape
    value_width = cotangent.shape[2]
    rank = adapter_down_factor.shape[1]
    depth, columns = projection.shape
    width = columns // side_count
    chunk = min(256, width)
    chunk_count = width // chunk
    own_ids = slots // side_count
    own_rank = rank // ctx_count
    block_lanes = max(LANES, own_rank * value_width // 16)
    block = -(-own_rank * value_width // block_lanes // 16) * 16
    assert example_count == 1 and depth == own_rank * value_width
    dma = pltpu.SemaphoreType.DMA
    return pl.pallas_call(
        functools.partial(kernel, sizes),
        out_shape=jax.ShapeDtypeStruct((own_ids, columns), F32),
        in_specs=[pl.BlockSpec(memory_space=pltpu.HBM)] * 6,
        out_specs=pl.BlockSpec(memory_space=pltpu.VMEM),
        scratch_shapes=[
            pltpu.SMEM(lengths.shape, jnp.int32),
            pltpu.SMEM(slot_example_order.shape, jnp.int32),
            pltpu.VMEM((token_count, model_width), BF16),
            pltpu.VMEM((token_count, value_width), BF16),
            pltpu.VMEM((rank, model_width), BF16),
            pltpu.VMEM((chunk_count, depth, chunk), BF16),
            pltpu.VMEM((group_count, 8, LANES), jnp.int32),
            pltpu.VMEM((ctx_count, block, block_lanes), F32),
            pltpu.VMEM((ctx_count, block, block_lanes), BF16),
            pltpu.VMEM((ctx_count, block, block_lanes), BF16),
            pltpu.VMEM((slots, block, block_lanes), BF16),
            pltpu.VMEM((chunk_count, slots * chunk // LANES, LANES), BF16),
            pltpu.VMEM((ctx_count, chunk_count, slots * chunk // LANES, LANES), BF16),
            pltpu.VMEM((side_count, chunk_count * own_ids, chunk + LANES), F32),
            pltpu.VMEM((side_count, chunk_count * own_ids, chunk + LANES), F32),
            pltpu.VMEM((slots, chunk_count * own_ids, LANES), F32),
            dma((4 + HIDDEN_CHUNKS,)),
            dma((chunk_count,)),
            dma((group_count,)),
            dma((group_count,)),
            dma((ctx_count,)),
            dma((ctx_count,)),
            dma((slots,)),
            dma((slots,)),
            dma((chunk_count, ctx_count)),
            dma((chunk_count, ctx_count)),
            dma((side_count,)),
            dma((side_count,)),
            dma(((feat_count - 1) * side_count,)),
            dma((slots,)),
        ],
        compiler_params=pltpu.CompilerParams(
            collective_id=0, has_side_effects=True, vmem_limit_bytes=215 * 1024 * 256
        ),
    )(lengths, slot_example_order, hidden, cotangent, adapter_down_factor.T, projection)


def solution(mesh):
    in_specs = (
        P(("group", "feat", "ex"), "ctx", None),
        P(("group", "feat", "ex"), "ctx", None),
        P(),
        P("ctx", "feat"),
        P(("group", "feat", "ex")),
        P("group"),
    )
    out_specs = P(("group", "ex"), "feat")
    sizes = (mesh.shape["group"], mesh.shape["ctx"], mesh.shape["feat"], mesh.shape["ex"])
    return jax.shard_map(
        functools.partial(per_device, sizes),
        mesh=mesh, in_specs=in_specs, out_specs=out_specs, check_vma=False,
    )
```

```python
import functools

import jax
import jax.numpy as jnp
from jax import lax
from jax.experimental import pallas as pl
from jax.experimental.pallas import tpu as pltpu
from jax.sharding import PartitionSpec as P

MESH = pl.DeviceIdType.MESH
F32 = jnp.float32
BF16 = jnp.bfloat16
LANES = 128
HIDDEN_CHUNKS = 4
PROJECTION_CHUNKS = 4


def loop(low, high, body):
    if high - low <= 8:
        for step in range(low, high):
            body(step)
    else:
        lax.fori_loop(low, high, lambda step, carry: (body(step), carry)[1], 0)


def kernel(
    sizes,
    lengths_ref, order_ref, hidden_ref, cotangent_ref, factor_ref, projection_ref,
    out_ref,
    lengths_v, order_v, hidden_v, cotangent_v, factor_v, projection_v,
    ids, partial, partial_in, grads, rows_out, rows_in, final_out, final_in, squares_in,
    local_sem, projection_sem, ids_send, ids_recv,
    grad_send, grad_recv, gather_send, gather_recv, rows_send, rows_recv,
    final_send, final_recv, squares_send, squares_recv,
):
    group_count, ctx_count, feat_count, ex_count = sizes
    group, ctx, feat = lax.axis_index("group"), lax.axis_index("ctx"), lax.axis_index("feat")
    ex = lax.axis_index("ex")
    side_count = group_count * ex_count
    side = group * ex_count + ex
    slots = feat_count * side_count
    slot = feat * side_count + side
    group_slots = feat_count * ex_count
    token_count, model_width = hidden_v.shape
    rank = factor_v.shape[0]
    own_rank = rank // ctx_count
    depth, width = projection_v.shape
    chunk_count = rows_out.shape[0]
    chunk = width // chunk_count
    value_width = cotangent_v.shape[1]
    padded = max(8, slots)
    own_ids = out_ref.shape[0]
    block, block_lanes = grads.shape[1:]
    pieces = value_width // block_lanes

    step = model_width // HIDDEN_CHUNKS
    factor_copy = pltpu.make_async_copy(factor_ref, factor_v, local_sem.at[0])
    factor_copy.start()

    def hidden_copy(k):
        columns = pl.ds(pl.multiple_of(k * step, LANES), step)
        return pltpu.make_async_copy(
            hidden_ref.at[0, :, columns], hidden_v.at[:, columns], local_sem.at[4 + k]
        )

    for k in range(HIDDEN_CHUNKS):
        hidden_copy(k).start()
    order_copy = pltpu.make_async_copy(order_ref, order_v, local_sem.at[2])
    order_copy.start()
    lengths_copy = pltpu.make_async_copy(lengths_ref, lengths_v, local_sem.at[3])
    lengths_copy.start()
    cotangent_copy = pltpu.make_async_copy(cotangent_ref.at[0], cotangent_v, local_sem.at[1])
    cotangent_copy.start()

    def projection_copy(k):
        rows = pl.ds(k * (depth // PROJECTION_CHUNKS), depth // PROJECTION_CHUNKS)
        columns = pl.ds(pl.multiple_of(side * width, LANES), width)
        return pltpu.make_async_copy(
            projection_ref.at[rows, columns], projection_v.at[rows], projection_sem.at[k]
        )

    def at_side(x):
        return {"group": x // ex_count, "ex": lax.rem(x, ex_count)}

    def ctx_peer(d):
        return lax.rem(ctx + d, ctx_count)

    def slot_peer(d):
        other = lax.rem(slot + d, slots)
        return other, {"feat": other // side_count, **at_side(lax.rem(other, side_count))}

    barrier = pltpu.get_barrier_semaphore()

    def greet_ctx(d):
        pl.semaphore_signal(
            barrier, inc=1, device_id_type=MESH, device_id={"ctx": ctx_peer(d)}
        )

    def greet_slot(d):
        pl.semaphore_signal(
            barrier, inc=1, device_id_type=MESH, device_id=slot_peer(d)[1]
        )

    loop(1, ctx_count, greet_ctx)
    loop(1, slots, greet_slot)

    order_copy.wait()
    lane = lax.broadcasted_iota(jnp.int32, ids.shape[1:], 1)
    own_order = jnp.zeros(ids.shape[1:], jnp.int32)
    for i in range(group_slots):
        own_order = jnp.where(lane == i, order_v[i], own_order)
    ids[group] = own_order

    lengths_copy.wait()
    factor_copy.wait()
    hidden_copy(0).wait()
    for k in range(PROJECTION_CHUNKS):
        projection_copy(k).start()

    def add_down(k, down):
        @pl.when(k > 0)
        def _():
            hidden_copy(k).wait()

        columns = pl.ds(pl.multiple_of(k * step, LANES), step)
        return down + lax.dot_general(
            factor_v[:, columns], hidden_v[:, columns], (((1,), (1,)), ((), ())),
            preferred_element_type=F32,
        )

    down = lax.fori_loop(0, HIDDEN_CHUNKS, add_down, jnp.zeros((rank, token_count), F32))
    position = ctx * token_count + lax.broadcasted_iota(jnp.int32, down.shape, 1)
    down = jnp.where(position < lengths_v[0], down, 0.0).astype(BF16)
    cotangent_copy.wait()
    grad = jnp.dot(down, cotangent_v[...], preferred_element_type=F32)
    for k in range(ctx_count):
        partial[k] = grad[k * own_rank:(k + 1) * own_rank]

    pl.semaphore_wait(barrier, ctx_count - 1 + slots - 1)

    def grad_copy(d, landing=None):
        other = ctx_peer(d)
        source = ctx if landing is None else other
        return pltpu.make_async_remote_copy(
            src_ref=partial.at[other], dst_ref=partial_in.at[source],
            send_sem=grad_send.at[d], recv_sem=grad_recv.at[source],
            device_id={"ctx": other}, device_id_type=MESH,
        )

    def ids_copy(d, landing=None):
        other = lax.rem(group + d, group_count)
        source = group if landing is None else other
        return pltpu.make_async_remote_copy(
            src_ref=ids.at[source], dst_ref=ids.at[source],
            send_sem=ids_send.at[d], recv_sem=ids_recv.at[source],
            device_id={"group": other}, device_id_type=MESH,
        )

    loop(1, ctx_count, lambda d: grad_copy(d).start())
    loop(1, group_count, lambda d: ids_copy(d).start())
    partial_in[ctx] = partial[ctx]

    loop(1, group_count, lambda d: ids_copy(d, True).wait_recv())
    pick_shape = (own_rank * pieces * padded, slots * block)
    row = lax.broadcasted_iota(jnp.int32, pick_shape, 0)
    column = lax.broadcasted_iota(jnp.int32, pick_shape, 1)
    column_id = jnp.zeros(pick_shape, jnp.int32)
    for f in range(feat_count):
        for x in range(side_count):
            i = f * ex_count + x % ex_count
            value = ids[x // ex_count, :1, i:i + 1] + (x // ex_count) * group_slots
            column_id = jnp.where(column // block == f * side_count + x, value, column_id)
    wanted = lax.rem(row // padded, pieces) * own_rank + row // (padded * pieces)
    pick = (lax.rem(column, block) == wanted) & (lax.rem(row, padded) == column_id)
    pick = pick.astype(F32).astype(BF16)

    loop(1, ctx_count, lambda d: grad_copy(d, True).wait_recv())
    total = partial_in[0]
    for k in range(1, ctx_count):
        total += partial_in[k]
    rows = [total[:, q * block_lanes:(q + 1) * block_lanes] for q in range(pieces)]
    if pieces * own_rank < block:
        rows.append(jnp.zeros((block - pieces * own_rank, block_lanes), F32))
    grads[slot] = jnp.concatenate(rows, axis=0).astype(BF16)

    def gather_copy(d, landing=None):
        other, device = slot_peer(d)
        source = slot if landing is None else other
        return pltpu.make_async_remote_copy(
            src_ref=grads.at[source], dst_ref=grads.at[source],
            send_sem=gather_send.at[d], recv_sem=gather_recv.at[source],
            device_id=device, device_id_type=MESH,
        )

    loop(1, slots, lambda d: gather_copy(d).start())
    loop(1, slots, lambda d: gather_copy(d, True).wait_recv())
    gathered = grads[...].reshape(slots * block, block_lanes)
    picked = jnp.dot(pick, gathered, preferred_element_type=F32)
    left = [picked[i * padded:(i + 1) * padded].astype(BF16) for i in range(own_rank * pieces)]

    def rows_copy(h, d, landing=None):
        other = ctx_peer(d)
        source = ctx if landing is None else other
        return pltpu.make_async_remote_copy(
            src_ref=rows_out.at[h], dst_ref=rows_in.at[source, h],
            send_sem=rows_send.at[h, d], recv_sem=rows_recv.at[h, source],
            device_id={"ctx": other}, device_id_type=MESH,
        )

    def project(k, carry):
        columns = pl.ds(pl.multiple_of(k * chunk, LANES), chunk)
        product = jnp.zeros((padded, chunk), F32)
        for i in range(own_rank * pieces):
            product += jnp.dot(
                left[i], projection_v[i * block_lanes:(i + 1) * block_lanes, columns],
                preferred_element_type=F32,
            )
        lanes = [product[:slots, p * LANES:(p + 1) * LANES] for p in range(chunk // LANES)]
        rows_out[k] = jnp.concatenate(lanes, axis=0).astype(BF16)
        for d in range(1, ctx_count):
            rows_copy(k, d).start()
        rows_in[ctx, k] = rows_out[k]
        return carry

    for k in range(PROJECTION_CHUNKS):
        projection_copy(k).wait()
    lax.fori_loop(0, chunk_count, project, 0)

    for k in range(chunk_count):
        loop(1, ctx_count, lambda d: rows_copy(k, d, True).wait_recv())
        summed = rows_in[0, k].astype(F32)
        for c in range(1, ctx_count):
            summed += rows_in[c, k].astype(F32)
        lanes = [summed[p * slots:(p + 1) * slots] for p in range(chunk // LANES)]
        square = lanes[0] * lanes[0]
        for part in lanes[1:]:
            square += part * part
        square = jnp.broadcast_to(jnp.sum(square, axis=1, keepdims=True), (slots, LANES))
        there = slice(k * own_ids, (k + 1) * own_ids)
        for x in range(side_count):
            here = slice(x * own_ids, (x + 1) * own_ids)
            for p, part in enumerate(lanes + [square]):
                final_out[x, there, p * LANES:(p + 1) * LANES] = part[here]

    tail = pl.ds(chunk, LANES)

    def final_copy(d, landing=None):
        other = lax.rem(side + d, side_count)
        source = side if landing is None else other
        return pltpu.make_async_remote_copy(
            src_ref=final_out.at[other], dst_ref=final_in.at[source],
            send_sem=final_send.at[d], recv_sem=final_recv.at[source],
            device_id=at_side(other), device_id_type=MESH,
        )

    def squares_copy(q, landing=None):
        g, x = q // side_count + 1, lax.rem(side + lax.rem(q, side_count), side_count)
        other = lax.rem(feat + g, feat_count)
        source = slot if landing is None else other * side_count + x
        return pltpu.make_async_remote_copy(
            src_ref=final_out.at[x, :, tail], dst_ref=squares_in.at[source],
            send_sem=squares_send.at[q], recv_sem=squares_recv.at[source],
            device_id={"feat": other, **at_side(x)}, device_id_type=MESH,
        )

    square_sends = (feat_count - 1) * side_count
    loop(0, square_sends, lambda q: squares_copy(q).start())
    loop(1, side_count, lambda d: final_copy(d).start())
    final_in[side] = final_out[side]
    loop(1, side_count, lambda d: final_copy(d, True).wait_recv())
    for x in range(side_count):
        squares_in[feat * side_count + x] = final_in[x, :, chunk:]
    loop(0, square_sends, lambda q: squares_copy(q, True).wait_recv())
    everything = squares_in[0]
    for s in range(1, slots):
        everything += squares_in[s]
    norm = everything[:own_ids, :1]
    for k in range(1, chunk_count):
        norm += everything[k * own_ids:(k + 1) * own_ids, :1]
    norm = jnp.sqrt(norm / (feat_count * side_count * width) + 1e-06)
    for x in range(side_count):
        for k in range(chunk_count):
            place = x * width + k * chunk
            out_ref[:, place:place + chunk] = final_in[x, k * own_ids:(k + 1) * own_ids, :chunk] / norm

    loop(1, ctx_count, lambda d: grad_copy(d).wait_send())
    loop(1, slots, lambda d: gather_copy(d).wait_send())
    for k in range(chunk_count):
        loop(1, ctx_count, lambda d: rows_copy(k, d).wait_send())
    loop(1, group_count, lambda d: ids_copy(d).wait_send())
    loop(1, side_count, lambda d: final_copy(d).wait_send())
    loop(0, square_sends, lambda q: squares_copy(q).wait_send())


def per_device(sizes, hidden, cotangent, adapter_down_factor, projection, lengths, slot_example_order):
    group_count, ctx_count, feat_count, ex_count = sizes
    side_count = group_count * ex_count
    slots = feat_count * side_count
    example_count, token_count, model_width = hidden.shape
    value_width = cotangent.shape[2]
    rank = adapter_down_factor.shape[1]
    depth, columns = projection.shape
    width = columns // side_count
    chunk = min(256, width)
    chunk_count = width // chunk
    own_ids = slots // side_count
    own_rank = rank // ctx_count
    block_lanes = max(LANES, own_rank * value_width // 16)
    block = -(-own_rank * value_width // block_lanes // 16) * 16
    assert example_count == 1 and depth == own_rank * value_width
    dma = pltpu.SemaphoreType.DMA
    return pl.pallas_call(
        functools.partial(kernel, sizes),
        out_shape=jax.ShapeDtypeStruct((own_ids, columns), F32),
        in_specs=[pl.BlockSpec(memory_space=pltpu.HBM)] * 6,
        out_specs=pl.BlockSpec(memory_space=pltpu.VMEM),
        scratch_shapes=[
            pltpu.SMEM(lengths.shape, jnp.int32),
            pltpu.SMEM(slot_example_order.shape, jnp.int32),
            pltpu.VMEM((token_count, model_width), BF16),
            pltpu.VMEM((token_count, value_width), BF16),
            pltpu.VMEM((rank, model_width), BF16),
            pltpu.VMEM((depth, width), BF16),
            pltpu.VMEM((group_count, 8, LANES), jnp.int32),
            pltpu.VMEM((ctx_count, own_rank, value_width), F32),
            pltpu.VMEM((ctx_count, own_rank, value_width), F32),
            pltpu.VMEM((slots, block, block_lanes), BF16),
            pltpu.VMEM((chunk_count, slots * chunk // LANES, LANES), BF16),
            pltpu.VMEM((ctx_count, chunk_count, slots * chunk // LANES, LANES), BF16),
            pltpu.VMEM((side_count, chunk_count * own_ids, chunk + LANES), F32),
            pltpu.VMEM((side_count, chunk_count * own_ids, chunk + LANES), F32),
            pltpu.VMEM((slots, chunk_count * own_ids, LANES), F32),
            dma((4 + HIDDEN_CHUNKS,)),
            dma((PROJECTION_CHUNKS,)),
            dma((group_count,)),
            dma((group_count,)),
            dma((ctx_count,)),
            dma((ctx_count,)),
            dma((slots,)),
            dma((slots,)),
            dma((chunk_count, ctx_count)),
            dma((chunk_count, ctx_count)),
            dma((side_count,)),
            dma((side_count,)),
            dma(((feat_count - 1) * side_count,)),
            dma((slots,)),
        ],
        compiler_params=pltpu.CompilerParams(
            collective_id=0, has_side_effects=True, vmem_limit_bytes=215 * 1024 * 256
        ),
    )(lengths, slot_example_order, hidden, cotangent, adapter_down_factor.T, projection)


def solution(mesh):
    in_specs = (
        P(("group", "feat", "ex"), "ctx", None),
        P(("group", "feat", "ex"), "ctx", None),
        P(),
        P("ctx", "feat"),
        P(("group", "feat", "ex")),
        P("group"),
    )
    out_specs = P(("group", "ex"), "feat")
    sizes = (mesh.shape["group"], mesh.shape["ctx"], mesh.shape["feat"], mesh.shape["ex"])
    return jax.shard_map(
        functools.partial(per_device, sizes),
        mesh=mesh, in_specs=in_specs, out_specs=out_specs, check_vma=False,
    )
```

```python
import functools

import jax
import jax.numpy as jnp
from jax import lax
from jax.experimental import pallas as pl
from jax.experimental.pallas import tpu as pltpu
from jax.sharding import PartitionSpec as P

MESH = pl.DeviceIdType.MESH
F32 = jnp.float32
BF16 = jnp.bfloat16
LANES = 128
HIDDEN_CHUNKS = 4


def loop(low, high, body):
    if high - low <= 8:
        for step in range(low, high):
            body(step)
    else:
        lax.fori_loop(low, high, lambda step, carry: (body(step), carry)[1], 0)


def kernel(
    sizes,
    lengths_ref, order_ref, hidden_ref, cotangent_ref, factor_ref, projection_ref,
    out_ref,
    lengths_v, order_v, hidden_v, cotangent_v, factor_v, projection_v,
    ids, partial, partial_in, grads, rows_out, rows_in, final_out, final_in, squares_in,
    local_sem, projection_sem, ids_send, ids_recv,
    grad_send, grad_recv, gather_send, gather_recv, rows_send, rows_recv,
    final_send, final_recv, squares_send, squares_recv,
):
    group_count, ctx_count, feat_count, ex_count = sizes
    group, ctx, feat = lax.axis_index("group"), lax.axis_index("ctx"), lax.axis_index("feat")
    ex = lax.axis_index("ex")
    side_count = group_count * ex_count
    side = group * ex_count + ex
    slots = feat_count * side_count
    slot = feat * side_count + side
    group_slots = feat_count * ex_count
    token_count, model_width = hidden_v.shape
    rank = factor_v.shape[0]
    own_rank = rank // ctx_count
    chunk_count, depth, chunk = projection_v.shape
    width = chunk_count * chunk
    value_width = cotangent_v.shape[1]
    padded = max(8, slots)
    own_ids = out_ref.shape[0]
    block, block_lanes = grads.shape[1:]
    pieces = value_width // block_lanes

    def at_side(x):
        return {"group": x // ex_count, "ex": lax.rem(x, ex_count)}

    def ctx_peer(d):
        return lax.rem(ctx + d, ctx_count)

    def slot_peer(d):
        other = lax.rem(slot + d, slots)
        return other, {"feat": other // side_count, **at_side(lax.rem(other, side_count))}

    barrier = pltpu.get_barrier_semaphore()

    def greet_ctx(d):
        pl.semaphore_signal(
            barrier, inc=1, device_id_type=MESH, device_id={"ctx": ctx_peer(d)}
        )

    def greet_slot(d):
        pl.semaphore_signal(
            barrier, inc=1, device_id_type=MESH, device_id=slot_peer(d)[1]
        )

    loop(1, ctx_count, greet_ctx)
    loop(1, slots, greet_slot)

    step = model_width // HIDDEN_CHUNKS
    factor_copy = pltpu.make_async_copy(factor_ref, factor_v, local_sem.at[0])
    factor_copy.start()

    def hidden_copy(k):
        columns = pl.ds(pl.multiple_of(k * step, LANES), step)
        return pltpu.make_async_copy(
            hidden_ref.at[0, :, columns], hidden_v.at[:, columns], local_sem.at[4 + k]
        )

    for k in range(HIDDEN_CHUNKS):
        hidden_copy(k).start()
    order_copy = pltpu.make_async_copy(order_ref, order_v, local_sem.at[2])
    order_copy.start()
    lengths_copy = pltpu.make_async_copy(lengths_ref, lengths_v, local_sem.at[3])
    lengths_copy.start()
    cotangent_copy = pltpu.make_async_copy(cotangent_ref.at[0], cotangent_v, local_sem.at[1])
    cotangent_copy.start()

    def projection_copy(k):
        columns = pl.ds(pl.multiple_of(side * width + k * chunk, LANES), chunk)
        return pltpu.make_async_copy(
            projection_ref.at[:, columns], projection_v.at[k], projection_sem.at[k]
        )

    order_copy.wait()
    lane = lax.broadcasted_iota(jnp.int32, ids.shape[1:], 1)
    own_order = jnp.zeros(ids.shape[1:], jnp.int32)
    for i in range(group_slots):
        own_order = jnp.where(lane == i, order_v[i], own_order)
    ids[group] = own_order

    lengths_copy.wait()
    factor_copy.wait()
    hidden_copy(0).wait()
    for k in range(chunk_count):
        projection_copy(k).start()

    def add_down(k, down):
        @pl.when(k > 0)
        def _():
            hidden_copy(k).wait()

        columns = pl.ds(pl.multiple_of(k * step, LANES), step)
        return down + lax.dot_general(
            factor_v[:, columns], hidden_v[:, columns], (((1,), (1,)), ((), ())),
            preferred_element_type=F32,
        )

    down = lax.fori_loop(0, HIDDEN_CHUNKS, add_down, jnp.zeros((rank, token_count), F32))
    position = ctx * token_count + lax.broadcasted_iota(jnp.int32, down.shape, 1)
    down = jnp.where(position < lengths_v[0], down, 0.0).astype(BF16)
    cotangent_copy.wait()
    grad = jnp.dot(down, cotangent_v[...], preferred_element_type=F32)
    for k in range(ctx_count):
        partial[k] = grad[k * own_rank:(k + 1) * own_rank]

    pl.semaphore_wait(barrier, ctx_count - 1 + slots - 1)

    def grad_copy(d, landing=None):
        other = ctx_peer(d)
        source = ctx if landing is None else other
        return pltpu.make_async_remote_copy(
            src_ref=partial.at[other], dst_ref=partial_in.at[source],
            send_sem=grad_send.at[d], recv_sem=grad_recv.at[source],
            device_id={"ctx": other}, device_id_type=MESH,
        )

    def ids_copy(d, landing=None):
        other = lax.rem(group + d, group_count)
        source = group if landing is None else other
        return pltpu.make_async_remote_copy(
            src_ref=ids.at[source], dst_ref=ids.at[source],
            send_sem=ids_send.at[d], recv_sem=ids_recv.at[source],
            device_id={"group": other}, device_id_type=MESH,
        )

    loop(1, ctx_count, lambda d: grad_copy(d).start())
    loop(1, group_count, lambda d: ids_copy(d).start())
    partial_in[ctx] = partial[ctx]

    loop(1, group_count, lambda d: ids_copy(d, True).wait_recv())
    pick_shape = (own_rank * pieces * padded, slots * block)
    row = lax.broadcasted_iota(jnp.int32, pick_shape, 0)
    column = lax.broadcasted_iota(jnp.int32, pick_shape, 1)
    column_id = jnp.zeros(pick_shape, jnp.int32)
    for f in range(feat_count):
        for x in range(side_count):
            i = f * ex_count + x % ex_count
            value = ids[x // ex_count, :1, i:i + 1] + (x // ex_count) * group_slots
            column_id = jnp.where(column // block == f * side_count + x, value, column_id)
    wanted = lax.rem(row // padded, pieces) * own_rank + row // (padded * pieces)
    pick = (lax.rem(column, block) == wanted) & (lax.rem(row, padded) == column_id)
    pick = pick.astype(F32).astype(BF16)

    loop(1, ctx_count, lambda d: grad_copy(d, True).wait_recv())
    total = partial_in[0]
    for k in range(1, ctx_count):
        total += partial_in[k]
    rows = [total[:, q * block_lanes:(q + 1) * block_lanes] for q in range(pieces)]
    if pieces * own_rank < block:
        rows.append(jnp.zeros((block - pieces * own_rank, block_lanes), F32))
    grads[slot] = jnp.concatenate(rows, axis=0).astype(BF16)

    def gather_copy(d, landing=None):
        other, device = slot_peer(d)
        source = slot if landing is None else other
        return pltpu.make_async_remote_copy(
            src_ref=grads.at[source], dst_ref=grads.at[source],
            send_sem=gather_send.at[d], recv_sem=gather_recv.at[source],
            device_id=device, device_id_type=MESH,
        )

    loop(1, slots, lambda d: gather_copy(d).start())
    loop(1, slots, lambda d: gather_copy(d, True).wait_recv())
    gathered = grads[...].reshape(slots * block, block_lanes)
    picked = jnp.dot(pick, gathered, preferred_element_type=F32)
    left = [picked[i * padded:(i + 1) * padded].astype(BF16) for i in range(own_rank * pieces)]

    def rows_copy(h, d, landing=None):
        other = ctx_peer(d)
        source = ctx if landing is None else other
        return pltpu.make_async_remote_copy(
            src_ref=rows_out.at[h], dst_ref=rows_in.at[source, h],
            send_sem=rows_send.at[h, d], recv_sem=rows_recv.at[h, source],
            device_id={"ctx": other}, device_id_type=MESH,
        )

    def project(k, carry):
        projection_copy(k).wait()
        product = jnp.zeros((padded, chunk), F32)
        for i in range(own_rank * pieces):
            product += jnp.dot(
                left[i], projection_v[k, i * block_lanes:(i + 1) * block_lanes, :],
                preferred_element_type=F32,
            )
        lanes = [product[:slots, p * LANES:(p + 1) * LANES] for p in range(chunk // LANES)]
        rows_out[k] = jnp.concatenate(lanes, axis=0).astype(BF16)
        for d in range(1, ctx_count):
            rows_copy(k, d).start()
        rows_in[ctx, k] = rows_out[k]
        return carry

    lax.fori_loop(0, chunk_count, project, 0)

    for k in range(chunk_count):
        loop(1, ctx_count, lambda d: rows_copy(k, d, True).wait_recv())
        summed = rows_in[0, k].astype(F32)
        for c in range(1, ctx_count):
            summed += rows_in[c, k].astype(F32)
        lanes = [summed[p * slots:(p + 1) * slots] for p in range(chunk // LANES)]
        square = lanes[0] * lanes[0]
        for part in lanes[1:]:
            square += part * part
        square = jnp.broadcast_to(jnp.sum(square, axis=1, keepdims=True), (slots, LANES))
        there = slice(k * own_ids, (k + 1) * own_ids)
        for x in range(side_count):
            here = slice(x * own_ids, (x + 1) * own_ids)
            for p, part in enumerate(lanes + [square]):
                final_out[x, there, p * LANES:(p + 1) * LANES] = part[here]

    tail = pl.ds(chunk, LANES)

    def final_copy(d, landing=None):
        other = lax.rem(side + d, side_count)
        source = side if landing is None else other
        return pltpu.make_async_remote_copy(
            src_ref=final_out.at[other], dst_ref=final_in.at[source],
            send_sem=final_send.at[d], recv_sem=final_recv.at[source],
            device_id=at_side(other), device_id_type=MESH,
        )

    def squares_copy(q, landing=None):
        g, x = q // side_count + 1, lax.rem(side + lax.rem(q, side_count), side_count)
        other = lax.rem(feat + g, feat_count)
        source = slot if landing is None else other * side_count + x
        return pltpu.make_async_remote_copy(
            src_ref=final_out.at[x, :, tail], dst_ref=squares_in.at[source],
            send_sem=squares_send.at[q], recv_sem=squares_recv.at[source],
            device_id={"feat": other, **at_side(x)}, device_id_type=MESH,
        )

    square_sends = (feat_count - 1) * side_count
    loop(1, side_count, lambda d: final_copy(d).start())
    loop(0, square_sends, lambda q: squares_copy(q).start())
    final_in[side] = final_out[side]
    loop(1, side_count, lambda d: final_copy(d, True).wait_recv())
    for x in range(side_count):
        squares_in[feat * side_count + x] = final_in[x, :, chunk:]
    loop(0, square_sends, lambda q: squares_copy(q, True).wait_recv())
    everything = squares_in[0]
    for s in range(1, slots):
        everything += squares_in[s]
    norm = everything[:own_ids, :1]
    for k in range(1, chunk_count):
        norm += everything[k * own_ids:(k + 1) * own_ids, :1]
    norm = jnp.sqrt(norm / (feat_count * side_count * width) + 1e-06)
    for x in range(side_count):
        for k in range(chunk_count):
            place = x * width + k * chunk
            out_ref[:, place:place + chunk] = final_in[x, k * own_ids:(k + 1) * own_ids, :chunk] / norm

    loop(1, ctx_count, lambda d: grad_copy(d).wait_send())
    loop(1, slots, lambda d: gather_copy(d).wait_send())
    for k in range(chunk_count):
        loop(1, ctx_count, lambda d: rows_copy(k, d).wait_send())
    loop(1, group_count, lambda d: ids_copy(d).wait_send())
    loop(1, side_count, lambda d: final_copy(d).wait_send())
    loop(0, square_sends, lambda q: squares_copy(q).wait_send())


def per_device(sizes, hidden, cotangent, adapter_down_factor, projection, lengths, slot_example_order):
    group_count, ctx_count, feat_count, ex_count = sizes
    side_count = group_count * ex_count
    slots = feat_count * side_count
    example_count, token_count, model_width = hidden.shape
    value_width = cotangent.shape[2]
    rank = adapter_down_factor.shape[1]
    depth, columns = projection.shape
    width = columns // side_count
    chunk = min(256, width)
    chunk_count = width // chunk
    own_ids = slots // side_count
    own_rank = rank // ctx_count
    block_lanes = max(LANES, own_rank * value_width // 16)
    block = -(-own_rank * value_width // block_lanes // 16) * 16
    assert example_count == 1 and depth == own_rank * value_width
    dma = pltpu.SemaphoreType.DMA
    return pl.pallas_call(
        functools.partial(kernel, sizes),
        out_shape=jax.ShapeDtypeStruct((own_ids, columns), F32),
        in_specs=[pl.BlockSpec(memory_space=pltpu.HBM)] * 6,
        out_specs=pl.BlockSpec(memory_space=pltpu.VMEM),
        scratch_shapes=[
            pltpu.SMEM(lengths.shape, jnp.int32),
            pltpu.SMEM(slot_example_order.shape, jnp.int32),
            pltpu.VMEM((token_count, model_width), BF16),
            pltpu.VMEM((token_count, value_width), BF16),
            pltpu.VMEM((rank, model_width), BF16),
            pltpu.VMEM((chunk_count, depth, chunk), BF16),
            pltpu.VMEM((group_count, 8, LANES), jnp.int32),
            pltpu.VMEM((ctx_count, own_rank, value_width), F32),
            pltpu.VMEM((ctx_count, own_rank, value_width), F32),
            pltpu.VMEM((slots, block, block_lanes), BF16),
            pltpu.VMEM((chunk_count, slots * chunk // LANES, LANES), BF16),
            pltpu.VMEM((ctx_count, chunk_count, slots * chunk // LANES, LANES), BF16),
            pltpu.VMEM((side_count, chunk_count * own_ids, chunk + LANES), F32),
            pltpu.VMEM((side_count, chunk_count * own_ids, chunk + LANES), F32),
            pltpu.VMEM((slots, chunk_count * own_ids, LANES), F32),
            dma((4 + HIDDEN_CHUNKS,)),
            dma((chunk_count,)),
            dma((group_count,)),
            dma((group_count,)),
            dma((ctx_count,)),
            dma((ctx_count,)),
            dma((slots,)),
            dma((slots,)),
            dma((chunk_count, ctx_count)),
            dma((chunk_count, ctx_count)),
            dma((side_count,)),
            dma((side_count,)),
            dma(((feat_count - 1) * side_count,)),
            dma((slots,)),
        ],
        compiler_params=pltpu.CompilerParams(
            collective_id=0, has_side_effects=True, vmem_limit_bytes=215 * 1024 * 256
        ),
    )(lengths, slot_example_order, hidden, cotangent, adapter_down_factor.T, projection)


def solution(mesh):
    in_specs = (
        P(("group", "feat", "ex"), "ctx", None),
        P(("group", "feat", "ex"), "ctx", None),
        P(),
        P("ctx", "feat"),
        P(("group", "feat", "ex")),
        P("group"),
    )
    out_specs = P(("group", "ex"), "feat")
    sizes = (mesh.shape["group"], mesh.shape["ctx"], mesh.shape["feat"], mesh.shape["ex"])
    return jax.shard_map(
        functools.partial(per_device, sizes),
        mesh=mesh, in_specs=in_specs, out_specs=out_specs, check_vma=False,
    )
```
